128 devices in a mesh: ex: 16 (over y, x), lay: 8 (over z, core).
Axes of the slice: x: 4, y: 4, z: 4, core: 2. Of those that a mesh axis runs over, the one named last changes fastest.
Arguments:
- grads: bfloat16 [8, 16384, 4096], P('lay', 'ex'), may hold values from -0.119628906 to 0.119628906
- prec_in: bfloat16 [8, 64, 64], P('lay'), as said below
- prec_out: bfloat16 [8, 64, 64], P('lay'), as said below
- requests: int32 [16, 16], replicated, may hold values from 0 to 7
- pairs: int32 [1024, 2], P('ex'), may hold values from 0 to 127, as said below
Outputs:
- gram: float32 [1024, 128, 128], P(('ex', 'lay'))
The draws below stay inside these ranges and needn't reach their ends.
Inputs may be any that keep to these rules, and one draw needn't show every extreme that they name: Each device's listed first blocks are its own: pairs[p, 0] lies in 8 * (p // 64) to 8 * (p // 64 + 1) - 1. pairs[p, 1] is a device number of ex. The 64 pairs of one device are distinct and name every device number at least once. `prec_in`: each matrix has a diagonal between 1.5 and 6 and exceeds the sum of magnitudes of the rest of its row. `prec_out`: each matrix has a diagonal between 1.5 and 6 and exceeds the sum of magnitudes of the rest of its row.
All inputs are finite; a program needn't handle non-finite values.
Results may differ from the reference program's by a relative error of at most 0.0026.
Values may be sent and summed in bfloat16 or wider, within the bound.
No kernel may reach another device: no remote copies, remote signals or barrier semaphores. Data moves between devices by JAX's collectives and lax.ppermute only.
A program may use at most 128 MiB of HBM per device.

```python
import jax
import jax.numpy as jnp
from jax import lax

RANK = 64
PROJ = 4096
BLOCK = 128
BLK_DEV = 8
PAIR_DEV = 64
LAYERS = 8
EXAMPLES = 16384
BLOCKS = 128
PAIRS = 1024


def factor_matrix(key):
    key_diag, key_off = jax.random.split(key)
    diag = jnp.exp(jax.random.uniform(key_diag, (LAYERS, RANK), jnp.float32, jnp.log(1.5), jnp.log(6.0)))
    bound = 1.45 / RANK
    off = jax.random.uniform(key_off, (LAYERS, RANK, RANK), jnp.float32, -bound, bound)
    off = 0.5 * (off + jnp.swapaxes(off, 1, 2))
    eye = jnp.eye(RANK, dtype=jnp.float32)
    return (off * (1.0 - eye) + diag[:, :, None] * eye).astype(jnp.bfloat16)


def draw_prec_in(key, part):
    return factor_matrix(jax.random.fold_in(key, 11))


def draw_prec_out(key, part):
    return factor_matrix(jax.random.fold_in(key, 23))


def draw_requests(key, part):
    devices = BLOCKS // BLK_DEV
    return jax.random.randint(jax.random.fold_in(key, 31), (devices, devices), 0, BLK_DEV).astype(jnp.int32)


def draw_pairs(key, part):
    devices = BLOCKS // BLK_DEV
    combos = BLK_DEV * devices
    keys = jax.random.split(jax.random.fold_in(key, 47), devices)
    combo_index = jnp.arange(combos, dtype=jnp.int32)
    local = combo_index // devices
    source = combo_index % devices

    def one_owner(owner_key, owner):
        key_forced, key_order = jax.random.split(owner_key)
        forced = jax.random.randint(key_forced, (devices,), 0, BLK_DEV).astype(jnp.int32)
        priority = (local != forced[source]).astype(jnp.int32)
        ranking = jax.random.permutation(key_order, combos).astype(jnp.int32)
        score = priority * combos + ranking
        order = jnp.argsort(score, stable=True)[:PAIR_DEV]
        first = owner * BLK_DEV + local[order]
        return jnp.stack([first, source[order]], axis=1).astype(jnp.int32)
    listed = jax.vmap(one_owner)(keys, jnp.arange(devices, dtype=jnp.int32))
    return listed.reshape(PAIRS, 2).astype(jnp.int32)


def block_levels(key, shape, shards, low, top_value):
    loudness = 1.0
    for axis_at, parts in shards:
        draws = jax.random.uniform(jax.random.fold_in(jax.random.fold_in(key, 6), axis_at), (parts,), jnp.float32, low / len(shards), top_value / len(shards))
        loudness = loudness * jnp.repeat(jnp.exp(draws), shape[axis_at] // parts).reshape((-1,) + (1,) * (len(shape) - 1 - axis_at))
    return loudness


def centred(stream_key, extent, deviation, most, pieces=(), kind=jnp.bfloat16):
    array = deviation * jax.random.normal(stream_key, extent, jnp.float32)
    if pieces:
        array = array * block_levels(stream_key, extent, pieces, -0.22, 0.18)
    return jnp.clip(array, -most, most).astype(kind)


def setup_inputs(seed: int = 0) -> dict:
    seeds = jax.random.split(jax.random.key(seed), 6)
    grads = centred(seeds[0], (LAYERS, EXAMPLES, PROJ), 0.02, 0.119628906, ((0, 8), (1, 16)))
    prec_in = draw_prec_in(jax.random.fold_in(seeds[5], 71), 0)
    prec_out = draw_prec_out(jax.random.fold_in(seeds[5], 71), 0)
    requests = draw_requests(jax.random.fold_in(seeds[5], 71), 0)
    pairs = draw_pairs(jax.random.fold_in(seeds[5], 71), 0)
    return {"grads": grads, "prec_in": prec_in, "prec_out": prec_out, "requests": requests, "pairs": pairs}


def precondition(block, prec_in, prec_out):
    square = block.astype(jnp.float32).reshape(block.shape[0], block.shape[1], RANK, RANK)
    inner = jnp.einsum('leoi,lij->leoj', square, prec_in.astype(jnp.float32), precision=lax.Precision.HIGHEST)
    inner = lax.optimization_barrier(inner.astype(jnp.bfloat16)).astype(jnp.float32)
    outer = jnp.einsum('lpo,leoj->lepj', prec_out.astype(jnp.float32), inner, precision=lax.Precision.HIGHEST)
    return outer.astype(jnp.bfloat16).reshape(block.shape)


def reference(grads, prec_in, prec_out, requests, pairs):
    def one_block(index):
        block = lax.dynamic_slice_in_dim(grads, index * BLOCK, BLOCK, 1)
        return precondition(block, prec_in, prec_out)

    prepared = lax.map(one_block, jnp.arange(BLOCKS, dtype=jnp.int32))
    owner = (jnp.arange(PAIRS, dtype=jnp.int32) // PAIR_DEV).astype(jnp.int32)

    def one_pair(item):
        pair, holder = item
        first = pair[0].astype(jnp.int32)
        source = pair[1].astype(jnp.int32)
        second = (source * BLK_DEV + requests[holder, source]).astype(jnp.int32)
        left = prepared[first]
        right = lax.dynamic_slice_in_dim(grads, second * BLOCK, BLOCK, 1)
        return jnp.einsum('lxp,lyp->xy', left.astype(jnp.float32), right.astype(jnp.float32), precision=lax.Precision.HIGHEST)

    return lax.map(one_pair, (pairs, owner))
```

```python
import functools

import jax
import jax.numpy as jnp
from jax import lax
from jax.experimental import pallas as pl
from jax.experimental.pallas import tpu as pltpu
from jax.sharding import PartitionSpec as P

BLOCK = 128
SIDE = 4
PARTS = ((0, 48), (96, 16))
VMEM = 60 * 2**20
bf16, f32 = jnp.bfloat16, jnp.float32


def params(limit=VMEM):
    return pltpu.CompilerParams(vmem_limit_bytes=limit)


def bundle_kernel(index_ref, block_ref, out_ref):
    out_ref[...] = block_ref[...]


def bundle(blocks, index, row, rows):
    count, width = index.shape[0], blocks.shape[-1]
    return pl.pallas_call(
        bundle_kernel,
        out_shape=jax.ShapeDtypeStruct((count, rows, width), blocks.dtype),
        grid_spec=pltpu.PrefetchScalarGridSpec(
            num_scalar_prefetch=1,
            grid=(count,),
            in_specs=[pl.BlockSpec((1, rows, width), lambda k, index: (index[k], row // rows, 0))],
            out_specs=pl.BlockSpec((1, rows, width), lambda k, index: (k, 0, 0)),
        ),
        compiler_params=params(8 * 2**20),
        cost_estimate=pl.CostEstimate(flops=0, bytes_accessed=4 * count * rows * width, transcendentals=0),
    )(index, blocks)


def left_kernel(rank, lanes, grads_ref, inner_w_ref, outer_w_ref, out_ref, inner_ref):
    group = inner_w_ref.shape[0]
    splits = rank // lanes
    per = group // splits
    width = grads_ref.shape[1]
    for g in range(width // group):
        part = grads_ref[:, g * group : (g + 1) * group]
        inner = lax.dot_general(
            inner_w_ref[...], part, (((1,), (1,)), ((), ())), preferred_element_type=f32
        ).astype(bf16)
        for s in range(splits):
            inner_ref[s, g * per : (g + 1) * per, :] = inner[s * per : (s + 1) * per]
    step = 256
    for s in range(splits):
        for at in range(0, rank * lanes, step):
            outer = jnp.dot(
                outer_w_ref[at : at + step, :], inner_ref[s], preferred_element_type=f32
            ).astype(bf16)
            for k in range(step // lanes):
                first = (at // lanes + k) * rank + s * lanes
                out_ref[first : first + lanes, :] = outer[k * lanes : (k + 1) * lanes]


def left_transposed(grads, prec_in, prec_out):
    examples, width = grads.shape
    rank = prec_in.shape[-1]
    lanes, outs, tile = 16, 4, 256
    splits = rank // lanes
    inner_w = jnp.einsum(
        "isj,oq->sojqi", prec_in.reshape(rank, splits, lanes), jnp.eye(outs, dtype=bf16)
    ).reshape(rank * outs, rank * outs)
    outer_w = jnp.einsum("po,jk->pjok", prec_out, jnp.eye(lanes, dtype=bf16)).reshape(
        rank * lanes, rank * lanes
    )
    return pl.pallas_call(
        functools.partial(left_kernel, rank, lanes),
        out_shape=jax.ShapeDtypeStruct((width, examples), bf16),
        grid=(examples // tile,),
        in_specs=[
            pl.BlockSpec((tile, width), lambda i: (i, 0)),
            pl.BlockSpec(inner_w.shape, lambda i: (0, 0)),
            pl.BlockSpec(outer_w.shape, lambda i: (0, 0)),
        ],
        out_specs=pl.BlockSpec((width, tile), lambda i: (0, i)),
        scratch_shapes=[pltpu.VMEM((splits, rank * lanes, tile), bf16)],
        compiler_params=params(),
        cost_estimate=pl.CostEstimate(
            flops=2 * examples * width * (rank * outs + rank * lanes),
            bytes_accessed=4 * examples * width,
            transcendentals=0,
        ),
    )(grads, inner_w, outer_w)


def tiles_kernel(count, block_ref, row_a_ref, row_b_ref, left_ref, *refs):
    rights, (keep_ref, give_ref, product_ref) = refs[:count], refs[count:]
    step = pl.program_id(0)
    per = left_ref.shape[1] // BLOCK
    at = 0
    for right_ref in rights:
        rows = right_ref.shape[0]
        product = jnp.dot(right_ref[...], left_ref[...], preferred_element_type=f32)
        for b in range(per):
            product_ref[step * per + b, at : at + rows, :] = product[:, b * BLOCK : (b + 1) * BLOCK]
        at += rows

    @pl.when(step == pl.num_programs(0) - 1)
    def _():
        half = keep_ref.shape[1] // 2
        for out_ref, base in ((keep_ref, 0), (give_ref, keep_ref.shape[0])):
            for q in range(out_ref.shape[0]):
                block = block_ref[base + q]
                row_a = pl.multiple_of(row_a_ref[base + q], 16)
                row_b = pl.multiple_of(row_b_ref[base + q], 16)
                out_ref[q, :half, :] = product_ref[block, pl.ds(row_a, half), :]
                out_ref[q, half:, :] = product_ref[block, pl.ds(row_b, half), :]


def tiles(left, rights, rows, block, row_a, row_b):
    width, examples = left.shape
    total = sum(r.shape[0] for r in rights)
    pairs = block.shape[0]
    step = 256
    out = jax.ShapeDtypeStruct((pairs // 2, 2 * rows, BLOCK), f32)
    out_spec = pl.BlockSpec(out.shape, lambda i, *_: (0, 0, 0))
    return pl.pallas_call(
        functools.partial(tiles_kernel, len(rights)),
        out_shape=(out, out),
        grid_spec=pltpu.PrefetchScalarGridSpec(
            num_scalar_prefetch=3,
            grid=(examples // step,),
            in_specs=[pl.BlockSpec((width, step), lambda i, *_: (0, i))]
            + [pl.BlockSpec(r.shape, lambda i, *_: (0, 0), pipeline_mode=pl.Buffered(1)) for r in rights],
            out_specs=(out_spec, out_spec),
            scratch_shapes=[pltpu.VMEM((examples // BLOCK, total, BLOCK), f32)],
        ),
        compiler_params=params(),
        cost_estimate=pl.CostEstimate(
            flops=2 * total * width * examples,
            bytes_accessed=2 * width * (examples + total),
            transcendentals=0,
        ),
    )(block, row_a, row_b, left, *rights)


def merge_kernel(keep_ref, got_ref, own_ref, *send_refs):
    per = own_ref.shape[0]
    own_ref[...] = keep_ref[:per] + got_ref[:per]
    for k, ref in enumerate(send_refs, 1):
        ref[...] = (keep_ref[k * per : (k + 1) * per] + got_ref[k * per : (k + 1) * per]).astype(bf16)


def merge(keep, got):
    shape = (keep.shape[0] // SIDE, *keep.shape[1:])
    return pl.pallas_call(
        merge_kernel,
        out_shape=(jax.ShapeDtypeStruct(shape, f32),)
        + (jax.ShapeDtypeStruct(shape, bf16),) * (SIDE - 1),
        compiler_params=params(32 * 2**20),
    )(keep, got)


def finish_kernel(*refs):
    ins, out_ref = refs[:-1], refs[-1]
    for k in range(out_ref.shape[0]):
        columns = []
        for at in range(0, len(ins), SIDE):
            total = ins[at][k]
            for ref in ins[at + 1 : at + SIDE]:
                total = total + ref[k].astype(f32)
            columns.append(total)
        out_ref[k] = jnp.concatenate(columns, axis=0).T


def finish(parts):
    ins = [x for part in parts for x in part]
    return pl.pallas_call(
        finish_kernel,
        out_shape=jax.ShapeDtypeStruct((ins[0].shape[0], BLOCK, BLOCK), f32),
        compiler_params=params(16 * 2**20),
    )(*ins)


def shift(array, dy, dx):
    pairs = [
        (y * SIDE + x, (y + dy) % SIDE * SIDE + (x + dx) % SIDE)
        for y in range(SIDE)
        for x in range(SIDE)
    ]
    return lax.ppermute(array, "ex", pairs)


def swap_cores(array):
    return lax.ppermute(array, "lay", [(i, i ^ 1) for i in range(2 * SIDE)])


def shift_z(array, dz):
    pairs = [(z * 2 + c, (z + dz) % SIDE * 2 + c) for z in range(SIDE) for c in range(2)]
    return lax.ppermute(array, "lay", pairs)


class Rounds:
    def __init__(self, window):
        self.done, self.window = [], window

    def __call__(self, *sends):
        ins = [s[0] for s in sends]
        if len(self.done) >= self.window:
            gate = self.done[-self.window]
            ins = lax.optimization_barrier((*ins, *gate))[: len(ins)]
        out = [shift(v, dy, dx) for v, (_, dy, dx) in zip(ins, sends)]
        self.done.append(out)
        return out


def turn(pieces):
    return [jnp.concatenate([p[k : k + 1] for p in pieces]) for k in range(SIDE)]


def on_device(grads, prec_in, prec_out, requests, pairs):
    grads, prec_in, prec_out = grads[0], prec_in[0], prec_out[0]
    examples, width = grads.shape
    block_count = examples // BLOCK
    blocks = grads.reshape(block_count, BLOCK, width)
    member, layer = lax.axis_index("ex"), lax.axis_index("lay")
    my_y, my_x = member // SIDE, member % SIDE
    my_z, my_core = layer // 2, layer % 2

    wanted = lax.dynamic_index_in_dim(requests, member, axis=1, keepdims=False).reshape(SIDE, SIDE)
    wanted = jnp.concatenate([wanted, wanted], 0)
    wanted = jnp.concatenate([wanted, wanted], 1)
    wanted = lax.dynamic_slice(wanted, (my_y, my_x), (SIDE, SIDE))

    rounds = Rounds(2)
    out_a, out_b, in_a, in_b = [], [], [], []
    for row, rows in PARTS:
        a = [bundle(blocks, wanted[d], row, rows) for d in range(SIDE)]
        b = [bundle(blocks, wanted[:, d], row + rows, rows) for d in range(SIDE)]
        a1, a3, b2 = rounds((a[1], 1, 0), (a[3], 3, 0), (b[2], 0, 2))
        b1, b3, a2 = rounds((b[1], 0, 1), (b[3], 0, 3), (a[2], 2, 0))
        out_a.append(turn([a[0], a1, a2, a3]))
        out_b.append(turn([b[0], b1, b2, b3]))
    for a, b in zip(out_a, out_b):
        a1, a3, b2 = rounds((a[1], 0, 1), (a[3], 0, 3), (b[2], 2, 0))
        b1, b3, a2 = rounds((b[1], 1, 0), (b[3], 3, 0), (a[2], 0, 2))
        in_a.append([a[0], a1, a2, a3])
        in_b.append([b[0], b1, b2, b3])

    left = left_transposed(grads, prec_in, prec_out)

    first = pairs[:, 0] - member * block_count
    dy = (my_y - pairs[:, 1] // SIDE) % SIDE
    dx = (my_x - pairs[:, 1] % SIDE) % SIDE
    listed = jnp.stack([first, dx * SIDE + dy, dy * SIDE + dx])
    listed = listed.reshape(3, SIDE, 2, -1)
    listed = jnp.concatenate([listed, listed], 1)
    listed = lax.dynamic_slice_in_dim(listed, my_z, SIDE, 1)
    listed = jnp.where(my_core == 0, listed, listed[:, :, ::-1])
    listed = listed.transpose(0, 2, 1, 3).reshape(3, -1)

    sums = []
    for (_, rows), a, b in zip(PARTS, in_a, in_b):
        rights = [r.reshape(SIDE * rows, width) for r in a + b]
        keep, give = tiles(
            left, rights, rows, listed[0], listed[1] * rows, (listed[2] + SIDE * SIDE) * rows
        )
        own, *sends = merge(keep, swap_cores(give))
        sums.append([own] + [shift_z(s, k) for k, s in enumerate(sends, 1)])
    return finish(sums)


def solution(mesh):
    placed = (P("lay", "ex", None), P("lay", None, None), P("lay", None, None), P(), P("ex", None))
    return jax.shard_map(
        on_device,
        mesh=mesh,
        in_specs=placed,
        out_specs=P(("ex", "lay"), None, None),
        check_vma=False,
    )
```

```python
import functools

import jax
import jax.numpy as jnp
from jax import lax
from jax.experimental import pallas as pl
from jax.experimental.pallas import tpu as pltpu
from jax.sharding import PartitionSpec as P

BLOCK = 128
SIDE = 4
PARTS = ((0, 48), (96, 16))
STEP = 256
VMEM = 60 * 2**20
bf16, f32 = jnp.bfloat16, jnp.float32


def params(limit=VMEM):
    return pltpu.CompilerParams(vmem_limit_bytes=limit)


def run_copies(copies):
    for copy in copies:
        copy.start()
    for copy in copies:
        copy.wait()


def moved(elements):
    return pl.CostEstimate(flops=0, bytes_accessed=4 * elements, transcendentals=0)


def gather_kernel(starts, index_ref, blocks_ref, *refs):
    outs, sems = refs[:-1], refs[-1]
    copies = []
    for n, (out_ref, start) in enumerate(zip(outs, starts)):
        count, rows = out_ref.shape[:2]
        for k in range(count):
            source = blocks_ref.at[index_ref[n * count + k], pl.ds(start, rows)]
            copies.append(pltpu.make_async_copy(source, out_ref.at[k], sems.at[n * count + k]))
    run_copies(copies)


def gather(blocks, bundles):
    width = blocks.shape[-1]
    outs = [jax.ShapeDtypeStruct((SIDE, rows, width), blocks.dtype) for _, _, rows in bundles]
    return pl.pallas_call(
        functools.partial(gather_kernel, [start for _, start, _ in bundles]),
        out_shape=outs,
        grid_spec=pltpu.PrefetchScalarGridSpec(
            num_scalar_prefetch=1,
            grid=(1,),
            in_specs=[pl.BlockSpec(memory_space=pl.ANY)],
            out_specs=[pl.BlockSpec(memory_space=pl.ANY)] * len(outs),
            scratch_shapes=[pltpu.SemaphoreType.DMA((SIDE * len(outs),))],
        ),
        compiler_params=params(),
        cost_estimate=moved(sum(SIDE * rows * width for _, _, rows in bundles)),
    )(jnp.concatenate([index for index, _, _ in bundles]), blocks)


def turn_kernel(*refs):
    pieces, outs, sems = refs[:SIDE], refs[SIDE:-1], refs[-1]
    copies = [
        pltpu.make_async_copy(piece.at[k + 1], out.at[i], sems.at[k * SIDE + i])
        for k, out in enumerate(outs)
        for i, piece in enumerate(pieces)
    ]
    run_copies(copies)


def turn(pieces):
    outs = [jax.ShapeDtypeStruct(pieces[0].shape, pieces[0].dtype)] * (SIDE - 1)
    return pl.pallas_call(
        turn_kernel,
        out_shape=outs,
        in_specs=[pl.BlockSpec(memory_space=pl.ANY)] * SIDE,
        out_specs=[pl.BlockSpec(memory_space=pl.ANY)] * (SIDE - 1),
        scratch_shapes=[pltpu.SemaphoreType.DMA((SIDE * (SIDE - 1),))],
        compiler_params=params(),
        cost_estimate=moved((SIDE - 1) * pieces[0].size),
    )(*pieces)


LANES = 16
OUTS = 4


def iota(shape, dim):
    return lax.broadcasted_iota(jnp.int32, shape, dim)


def one_hot(picked, shape):
    return (picked == iota(shape, 1)).astype(f32).astype(bf16)


def left_kernel(grads_ref, prec_in_ref, prec_out_ref, out_ref, inner_w_ref, outer_w_ref, inner_ref):
    rank = prec_in_ref.shape[0]
    group = rank * OUTS
    splits = rank // LANES
    per = group // splits
    width = grads_ref.shape[1]
    step = 256

    @pl.when(pl.program_id(0) == 0)
    def _():
        row = iota((group, rank), 0)
        rows = one_hot(row // per * LANES + row % LANES, (group, rank))
        columns = one_hot(row % rank, (group, rank))
        spread = lax.dot_general(
            rows, prec_in_ref[...], (((1,), (1,)), ((), ())), preferred_element_type=f32
        ).astype(bf16)
        full = lax.dot_general(spread, columns, (((1,), (1,)), ((), ())), preferred_element_type=f32)
        same = iota((group, group), 0) % per // LANES == iota((group, group), 1) // rank
        inner_w_ref[...] = jnp.where(same, full, 0.0).astype(bf16)
        columns = one_hot(iota((rank * LANES, rank), 0) // LANES, (rank * LANES, rank))
        for at in range(0, rank * LANES, step):
            rows = one_hot((iota((step, rank), 0) + at) // LANES, (step, rank))
            spread = jnp.dot(rows, prec_out_ref[...], preferred_element_type=f32).astype(bf16)
            full = lax.dot_general(spread, columns, (((1,), (1,)), ((), ())), preferred_element_type=f32)
            shape = (step, rank * LANES)
            same = iota(shape, 0) % LANES == iota(shape, 1) % LANES
            outer_w_ref[at : at + step, :] = jnp.where(same, full, 0.0).astype(bf16)

    for g in range(width // group):
        part = grads_ref[:, g * group : (g + 1) * group]
        inner = lax.dot_general(
            inner_w_ref[...], part, (((1,), (1,)), ((), ())), preferred_element_type=f32
        ).astype(bf16)
        for s in range(splits):
            inner_ref[s, g * per : (g + 1) * per, :] = inner[s * per : (s + 1) * per]
    for s in range(splits):
        for at in range(0, rank * LANES, step):
            outer = jnp.dot(
                outer_w_ref[at : at + step, :], inner_ref[s], preferred_element_type=f32
            ).astype(bf16)
            for k in range(step // LANES):
                first = (at // LANES + k) * rank + s * LANES
                out_ref[0, first : first + LANES, :] = outer[k * LANES : (k + 1) * LANES]


def left_transposed(grads, prec_in, prec_out):
    examples, width = grads.shape
    rank = prec_in.shape[-1]
    tile = STEP
    factor = pl.BlockSpec((rank, rank), lambda i: (0, 0))
    return pl.pallas_call(
        left_kernel,
        out_shape=jax.ShapeDtypeStruct((examples // tile, width, tile), bf16),
        grid=(examples // tile,),
        in_specs=[pl.BlockSpec((tile, width), lambda i: (i, 0)), factor, factor],
        out_specs=pl.BlockSpec((1, width, tile), lambda i: (i, 0, 0)),
        scratch_shapes=[
            pltpu.VMEM((rank * OUTS, rank * OUTS), bf16),
            pltpu.VMEM((rank * LANES, rank * LANES), bf16),
            pltpu.VMEM((rank // LANES, rank * LANES, tile), bf16),
        ],
        compiler_params=params(),
        cost_estimate=pl.CostEstimate(
            flops=2 * examples * width * (rank * OUTS + rank * LANES),
            bytes_accessed=4 * examples * width,
            transcendentals=0,
        ),
    )(grads, prec_in, prec_out)


def fetch(rights, right_ref, sems):
    copies, at = [], 0
    for k, ref in enumerate(rights):
        rows = ref.shape[0]
        copies.append(pltpu.make_async_copy(ref, right_ref.at[pl.ds(at, rows)], sems.at[k]))
        at += rows
    run_copies(copies)


def multiply(right_ref, left_ref, product_ref, first_block, at):
    rows = right_ref.shape[0]
    product = jnp.dot(right_ref[...], left_ref[0], preferred_element_type=f32)
    for b in range(left_ref.shape[2] // BLOCK):
        product_ref[first_block + b, at : at + rows, :] = product[:, b * BLOCK : (b + 1) * BLOCK]


def early_kernel(owns, count, left_ref, *refs):
    rights, (out_ref, right_ref, sems) = refs[:count], refs[count:]
    rights = [ref.at[0] for ref in rights[:owns]] + [ref for ref in rights[owns:]]

    @pl.when(pl.program_id(0) == 0)
    def _():
        fetch(rights, right_ref, sems)

    multiply(right_ref, left_ref, out_ref, 0, 0)


def cost(total, width, examples):
    return pl.CostEstimate(
        flops=2 * total * width * examples,
        bytes_accessed=2 * width * (examples + total) + 4 * total * examples,
        transcendentals=0,
    )


def early_products(left, owns, rights):
    groups, width, _ = left.shape
    examples = groups * STEP
    rows = owns[0].shape[1]
    total = rows * len(owns) + sum(r.shape[0] for r in rights)
    owned, rights = len(owns), [*owns, *rights]
    return pl.pallas_call(
        functools.partial(early_kernel, owned, len(rights)),
        out_shape=jax.ShapeDtypeStruct((examples // BLOCK, total, BLOCK), f32),
        grid=(examples // STEP,),
        in_specs=[pl.BlockSpec((1, width, STEP), lambda i: (i, 0, 0))]
        + [pl.BlockSpec(memory_space=pl.ANY)] * len(rights),
        out_specs=pl.BlockSpec((STEP // BLOCK, total, BLOCK), lambda i: (i, 0, 0)),
        scratch_shapes=[
            pltpu.VMEM((total, width), bf16),
            pltpu.SemaphoreType.DMA((len(rights),)),
        ],
        compiler_params=params(),
        cost_estimate=cost(total, width, examples),
    )(left, *rights)


def tiles_kernel(count, block_ref, row_a_ref, row_b_ref, left_ref, early_ref, *refs):
    rights = refs[:count]
    keep_ref, give_ref, product_ref, right_ref, sems, early_sem = refs[count:]
    step = pl.program_id(0)
    early = early_ref.shape[1]
    early_copy = pltpu.make_async_copy(early_ref, product_ref.at[:, pl.ds(0, early)], early_sem)

    @pl.when(step == 0)
    def _():
        early_copy.start()
        fetch(rights, right_ref, sems)

    multiply(right_ref, left_ref, product_ref, step * (left_ref.shape[2] // BLOCK), early)

    @pl.when(step == pl.num_programs(0) - 1)
    def _():
        early_copy.wait()
        half = keep_ref.shape[1] // 2
        for out_ref, base in ((give_ref, keep_ref.shape[0]), (keep_ref, 0)):
            for q in range(out_ref.shape[0]):
                block = block_ref[base + q]
                row_a = pl.multiple_of(row_a_ref[base + q], 16)
                row_b = pl.multiple_of(row_b_ref[base + q], 16)
                out_ref[q, :half, :] = product_ref[block, pl.ds(row_a, half), :]
                out_ref[q, half:, :] = product_ref[block, pl.ds(row_b, half), :]


def tiles(left, early, rights, rows, block, row_a, row_b):
    groups, width, _ = left.shape
    examples = groups * STEP
    total = sum(r.shape[0] for r in rights)
    pairs = block.shape[0]
    out = jax.ShapeDtypeStruct((pairs // 2, 2 * rows, BLOCK), f32)
    out_spec = pl.BlockSpec(out.shape, lambda i, *_: (0, 0, 0))
    return pl.pallas_call(
        functools.partial(tiles_kernel, len(rights)),
        out_shape=(out, out),
        grid_spec=pltpu.PrefetchScalarGridSpec(
            num_scalar_prefetch=3,
            grid=(examples // STEP,),
            in_specs=[pl.BlockSpec((1, width, STEP), lambda i, *_: (i, 0, 0))]
            + [pl.BlockSpec(memory_space=pl.ANY)] * (1 + len(rights)),
            out_specs=(out_spec, out_spec),
            scratch_shapes=[
                pltpu.VMEM((examples // BLOCK, early.shape[1] + total, BLOCK), f32),
                pltpu.VMEM((total, width), bf16),
                pltpu.SemaphoreType.DMA((len(rights),)),
                pltpu.SemaphoreType.DMA(()),
            ],
        ),
        compiler_params=params(),
        cost_estimate=cost(total, width, examples),
    )(block, row_a, row_b, left, early, *rights)


def merge_kernel(keep_ref, got_ref, own_ref, *send_refs):
    per = own_ref.shape[0]
    own_ref[...] = keep_ref[:per] + got_ref[:per]
    for k, ref in enumerate(send_refs, 1):
        ref[...] = (keep_ref[k * per : (k + 1) * per] + got_ref[k * per : (k + 1) * per]).astype(bf16)


def merge(keep, got):
    shape = (keep.shape[0] // SIDE, *keep.shape[1:])
    return pl.pallas_call(
        merge_kernel,
        out_shape=(jax.ShapeDtypeStruct(shape, f32),)
        + (jax.ShapeDtypeStruct(shape, bf16),) * (SIDE - 1),
        compiler_params=params(32 * 2**20),
    )(keep, got)


def finish_kernel(*refs):
    ins, out_ref = refs[:-1], refs[-1]
    for k in range(out_ref.shape[0]):
        columns = []
        for at in range(0, len(ins), SIDE):
            total = ins[at][k]
            for ref in ins[at + 1 : at + SIDE]:
                total = total + ref[k].astype(f32)
            columns.append(total)
        out_ref[k] = jnp.concatenate(columns, axis=0).T


def finish(parts):
    ins = [x for part in parts for x in part]
    return pl.pallas_call(
        finish_kernel,
        out_shape=jax.ShapeDtypeStruct((ins[0].shape[0], BLOCK, BLOCK), f32),
        compiler_params=params(16 * 2**20),
    )(*ins)


def shift(array, dy, dx):
    pairs = [
        (y * SIDE + x, (y + dy) % SIDE * SIDE + (x + dx) % SIDE)
        for y in range(SIDE)
        for x in range(SIDE)
    ]
    return lax.ppermute(array, "ex", pairs)


def swap_cores(array):
    return lax.ppermute(array, "lay", [(i, i ^ 1) for i in range(2 * SIDE)])


def shift_z(array, dz):
    pairs = [(z * 2 + c, (z + dz) % SIDE * 2 + c) for z in range(SIDE) for c in range(2)]
    return lax.ppermute(array, "lay", pairs)


IN_FLIGHT = 5


class Sender:
    def __init__(self):
        self.done = []

    def __call__(self, array, dy, dx):
        if len(self.done) >= IN_FLIGHT:
            array, _ = lax.optimization_barrier((array, self.done[-IN_FLIGHT]))
        self.done.append(shift(array, dy, dx))
        return self.done[-1]


def on_device(grads, prec_in, prec_out, requests, pairs):
    grads, prec_in, prec_out = grads[0], prec_in[0], prec_out[0]
    examples, width = grads.shape
    block_count = examples // BLOCK
    blocks = grads.reshape(block_count, BLOCK, width)
    member, layer = lax.axis_index("ex"), lax.axis_index("lay")
    my_y, my_x = member // SIDE, member % SIDE
    my_z, my_core = layer // 2, layer % 2

    wanted = lax.dynamic_index_in_dim(requests, member, axis=1, keepdims=False).reshape(SIDE, SIDE)
    wanted = jnp.concatenate([wanted, wanted], 0)
    wanted = jnp.concatenate([wanted, wanted], 1)
    wanted = lax.dynamic_slice(wanted, (my_y, my_x), (SIDE, SIDE))

    send = Sender()
    need = [(0, 1), (0, 3), (1, 2), (1, 1), (1, 3), (0, 2), (0, 0), (1, 0)]
    out = []
    for row, rows in PARTS:
        listed = [
            (wanted[:, d] if f else wanted[d], row + f * rows, rows) for f, d in need
        ]
        out.append(listed)
    calls = [out[0][:3], out[0][3:6], out[0][6:] + out[1]]
    made = [v for call in calls for v in gather(blocks, call)]
    parts = []
    for p in range(len(PARTS)):
        got = dict(zip(need, made[p * len(need) : (p + 1) * len(need)]))
        for f, d in need[:6]:
            got[f, d] = send(got[f, d], 0 if f else d, d if f else 0)
        parts.append([[got[f, d] for d in range(SIDE)] for f in range(2)])
    late_in = []
    for a, b in parts:
        sides = [turn(a), turn(b)]
        got = {}
        for f, d in need[:6]:
            got[f, d] = send(sides[f][d - 1], d if f else 0, 0 if f else d)
        late_in.append(got)

    left = left_transposed(grads, prec_in, prec_out)

    own, early, late = need[6:], need[:3], need[3:6]
    order = own + early + late

    def place(f, d):
        return sum(jnp.where(d == k, at, 0) for at, (n, k) in enumerate(order) if n == f)

    first = pairs[:, 0] - member * block_count
    dy = (my_y - pairs[:, 1] // SIDE) % SIDE
    dx = (my_x - pairs[:, 1] % SIDE) % SIDE
    listed = jnp.stack([first, place(0, dx) * SIDE + dy, place(1, dy) * SIDE + dx])
    listed = listed.reshape(3, SIDE, 2, -1)
    listed = jnp.concatenate([listed, listed], 1)
    listed = lax.dynamic_slice_in_dim(listed, my_z, SIDE, 1)
    listed = jnp.where(my_core == 0, listed, listed[:, :, ::-1])
    listed = listed.transpose(0, 2, 1, 3).reshape(3, -1)

    sums = []
    for (_, rows), sides, got in zip(PARTS, parts, late_in):
        flat = {key: got[key].reshape(-1, width) for key in early + late}
        owns = [piece for f, _ in own for piece in sides[f]]
        products = early_products(left, owns, [flat[key] for key in early])
        rest = [flat[key] for key in late]
        if sums:
            *rest, _ = lax.optimization_barrier((*rest, sums[-1]))
        keep, give = tiles(left, products, rest, rows, listed[0], listed[1] * rows, listed[2] * rows)
        mine, *sends = merge(keep, swap_cores(give))
        sums.append([mine] + [shift_z(s, k) for k, s in enumerate(sends, 1)])
    return finish(sums)


def solution(mesh):
    placed = (P("lay", "ex", None), P("lay", None, None), P("lay", None, None), P(), P("ex", None))
    return jax.shard_map(
        on_device,
        mesh=mesh,
        in_specs=placed,
        out_specs=P(("ex", "lay"), None, None),
        check_vma=False,
    )
```

```python
import functools

import jax
import jax.numpy as jnp
from jax import lax
from jax.experimental import pallas as pl
from jax.experimental.pallas import tpu as pltpu
from jax.sharding import PartitionSpec as P

BLOCK = 128
SIDE = 4
PARTS = ((0, 48), (96, 16))
STEP = 256
VMEM = 60 * 2**20
bf16, f32 = jnp.bfloat16, jnp.float32


def params(limit=VMEM):
    return pltpu.CompilerParams(vmem_limit_bytes=limit)


def run_copies(copies):
    for copy in copies:
        copy.start()
    for copy in copies:
        copy.wait()


def relay(pieces, sems):
    ins = [pltpu.make_async_copy(src, mid, sems.at[0, k]) for k, (src, mid, _) in enumerate(pieces)]
    outs = [pltpu.make_async_copy(mid, dst, sems.at[1, k]) for k, (_, mid, dst) in enumerate(pieces)]
    for copy in ins:
        copy.start()
    for arrived, copy in zip(ins, outs):
        arrived.wait()
        copy.start()
    for copy in outs:
        copy.wait()


def relay_scratch(outs):
    return [pltpu.VMEM(o.shape, o.dtype) for o in outs] + [
        pltpu.SemaphoreType.DMA((2, SIDE * len(outs)))
    ]


def moved(elements):
    return pl.CostEstimate(flops=0, bytes_accessed=4 * elements, transcendentals=0)


def gather_kernel(starts, index_ref, blocks_ref, *refs):
    n = len(starts)
    outs, mids, sems = refs[:n], refs[n : 2 * n], refs[2 * n]
    pieces = []
    for at, start in enumerate(starts):
        rows = outs[at].shape[1]
        for k in range(SIDE):
            source = blocks_ref.at[index_ref[at * SIDE + k], pl.ds(start, rows)]
            pieces.append((source, mids[at].at[k], outs[at].at[k]))
    relay(pieces, sems)


def gather(blocks, bundles):
    width = blocks.shape[-1]
    outs = [jax.ShapeDtypeStruct((SIDE, rows, width), blocks.dtype) for _, _, rows in bundles]
    return pl.pallas_call(
        functools.partial(gather_kernel, [start for _, start, _ in bundles]),
        out_shape=outs,
        grid_spec=pltpu.PrefetchScalarGridSpec(
            num_scalar_prefetch=1,
            grid=(1,),
            in_specs=[pl.BlockSpec(memory_space=pl.ANY)],
            out_specs=[pl.BlockSpec(memory_space=pl.ANY)] * len(outs),
            scratch_shapes=relay_scratch(outs),
        ),
        compiler_params=params(),
        cost_estimate=moved(sum(SIDE * rows * width for _, _, rows in bundles)),
    )(jnp.concatenate([index for index, _, _ in bundles]), blocks)


def turn_kernel(*refs):
    n = SIDE - 1
    ins, outs, mids, sems = refs[:SIDE], refs[SIDE : SIDE + n], refs[SIDE + n : SIDE + 2 * n], refs[-1]
    pieces = [
        (ins[i].at[k + 1], mids[k].at[i], outs[k].at[i]) for k in range(n) for i in range(SIDE)
    ]
    relay(pieces, sems)


def turn(pieces):
    outs = [jax.ShapeDtypeStruct(pieces[0].shape, pieces[0].dtype)] * (SIDE - 1)
    return pl.pallas_call(
        turn_kernel,
        out_shape=outs,
        in_specs=[pl.BlockSpec(memory_space=pl.ANY)] * SIDE,
        out_specs=[pl.BlockSpec(memory_space=pl.ANY)] * (SIDE - 1),
        scratch_shapes=relay_scratch(outs),
        compiler_params=params(),
        cost_estimate=moved((SIDE - 1) * pieces[0].size),
    )(*pieces)


LANES = 16
OUTS = 4


def iota(shape, dim):
    return lax.broadcasted_iota(jnp.int32, shape, dim)


def one_hot(picked, shape):
    return (picked == iota(shape, 1)).astype(f32).astype(bf16)


def left_kernel(grads_ref, prec_in_ref, prec_out_ref, out_ref, inner_w_ref, outer_w_ref, inner_ref):
    rank = prec_in_ref.shape[0]
    group = rank * OUTS
    splits = rank // LANES
    per = group // splits
    width = grads_ref.shape[1]
    step = 256

    @pl.when(pl.program_id(0) == 0)
    def _():
        row = iota((group, rank), 0)
        rows = one_hot(row // per * LANES + row % LANES, (group, rank))
        columns = one_hot(row % rank, (group, rank))
        spread = lax.dot_general(
            rows, prec_in_ref[...], (((1,), (1,)), ((), ())), preferred_element_type=f32
        ).astype(bf16)
        full = lax.dot_general(spread, columns, (((1,), (1,)), ((), ())), preferred_element_type=f32)
        same = iota((group, group), 0) % per // LANES == iota((group, group), 1) // rank
        inner_w_ref[...] = jnp.where(same, full, 0.0).astype(bf16)
        columns = one_hot(iota((rank * LANES, rank), 0) // LANES, (rank * LANES, rank))
        for at in range(0, rank * LANES, step):
            rows = one_hot((iota((step, rank), 0) + at) // LANES, (step, rank))
            spread = jnp.dot(rows, prec_out_ref[...], preferred_element_type=f32).astype(bf16)
            full = lax.dot_general(spread, columns, (((1,), (1,)), ((), ())), preferred_element_type=f32)
            shape = (step, rank * LANES)
            same = iota(shape, 0) % LANES == iota(shape, 1) % LANES
            outer_w_ref[at : at + step, :] = jnp.where(same, full, 0.0).astype(bf16)

    for g in range(width // group):
        part = grads_ref[:, g * group : (g + 1) * group]
        inner = lax.dot_general(
            inner_w_ref[...], part, (((1,), (1,)), ((), ())), preferred_element_type=f32
        ).astype(bf16)
        for s in range(splits):
            inner_ref[s, g * per : (g + 1) * per, :] = inner[s * per : (s + 1) * per]
    for s in range(splits):
        for at in range(0, rank * LANES, step):
            outer = jnp.dot(
                outer_w_ref[at : at + step, :], inner_ref[s], preferred_element_type=f32
            ).astype(bf16)
            for k in range(step // LANES):
                first = (at // LANES + k) * rank + s * LANES
                out_ref[0, first : first + LANES, :] = outer[k * LANES : (k + 1) * LANES]


def left_transposed(grads, prec_in, prec_out):
    examples, width = grads.shape
    rank = prec_in.shape[-1]
    tile = STEP
    factor = pl.BlockSpec((rank, rank), lambda i: (0, 0))
    return pl.pallas_call(
        left_kernel,
        out_shape=jax.ShapeDtypeStruct((examples // tile, width, tile), bf16),
        grid=(examples // tile,),
        in_specs=[pl.BlockSpec((tile, width), lambda i: (i, 0)), factor, factor],
        out_specs=pl.BlockSpec((1, width, tile), lambda i: (i, 0, 0)),
        scratch_shapes=[
            pltpu.VMEM((rank * OUTS, rank * OUTS), bf16),
            pltpu.VMEM((rank * LANES, rank * LANES), bf16),
            pltpu.VMEM((rank // LANES, rank * LANES, tile), bf16),
        ],
        compiler_params=params(),
        cost_estimate=pl.CostEstimate(
            flops=2 * examples * width * (rank * OUTS + rank * LANES),
            bytes_accessed=4 * examples * width,
            transcendentals=0,
        ),
    )(grads, prec_in, prec_out)


def fetch(rights, right_ref, sems):
    copies, at = [], 0
    for k, ref in enumerate(rights):
        rows = ref.shape[0]
        copies.append(pltpu.make_async_copy(ref, right_ref.at[pl.ds(at, rows)], sems.at[k]))
        at += rows
    run_copies(copies)


def multiply(right_ref, left_ref, product_ref, first_block, at):
    rows = right_ref.shape[0]
    product = jnp.dot(right_ref[...], left_ref[0], preferred_element_type=f32)
    for b in range(left_ref.shape[2] // BLOCK):
        product_ref[first_block + b, at : at + rows, :] = product[:, b * BLOCK : (b + 1) * BLOCK]


def early_kernel(owns, count, left_ref, *refs):
    rights, (out_ref, right_ref, sems) = refs[:count], refs[count:]
    rights = [ref.at[0] for ref in rights[:owns]] + [ref for ref in rights[owns:]]

    @pl.when(pl.program_id(0) == 0)
    def _():
        fetch(rights, right_ref, sems)

    multiply(right_ref, left_ref, out_ref, 0, 0)


def cost(total, width, examples):
    return pl.CostEstimate(
        flops=2 * total * width * examples,
        bytes_accessed=2 * width * (examples + total) + 4 * total * examples,
        transcendentals=0,
    )


def early_products(left, owns, rights):
    groups, width, _ = left.shape
    examples = groups * STEP
    rows = owns[0].shape[1]
    total = rows * len(owns) + sum(r.shape[0] for r in rights)
    owned, rights = len(owns), [*owns, *rights]
    return pl.pallas_call(
        functools.partial(early_kernel, owned, len(rights)),
        out_shape=jax.ShapeDtypeStruct((examples // BLOCK, total, BLOCK), f32),
        grid=(examples // STEP,),
        in_specs=[pl.BlockSpec((1, width, STEP), lambda i: (i, 0, 0))]
        + [pl.BlockSpec(memory_space=pl.ANY)] * len(rights),
        out_specs=pl.BlockSpec((STEP // BLOCK, total, BLOCK), lambda i: (i, 0, 0)),
        scratch_shapes=[
            pltpu.VMEM((total, width), bf16),
            pltpu.SemaphoreType.DMA((len(rights),)),
        ],
        compiler_params=params(32 * 2**20),
        cost_estimate=cost(total, width, examples),
    )(left, *rights)


def tiles_kernel(count, block_ref, row_a_ref, row_b_ref, left_ref, early_ref, *refs):
    rights = refs[:count]
    keep_ref, give_ref, product_ref, right_ref, sems, early_sem = refs[count:]
    step = pl.program_id(0)
    early = early_ref.shape[1]
    early_copy = pltpu.make_async_copy(early_ref, product_ref.at[:, pl.ds(0, early)], early_sem)

    @pl.when(step == 0)
    def _():
        early_copy.start()
        fetch(rights, right_ref, sems)

    multiply(right_ref, left_ref, product_ref, step * (left_ref.shape[2] // BLOCK), early)

    @pl.when(step == pl.num_programs(0) - 1)
    def _():
        early_copy.wait()
        half = keep_ref.shape[1] // 2
        for out_ref, base in ((give_ref, keep_ref.shape[0]), (keep_ref, 0)):
            for q in range(out_ref.shape[0]):
                block = block_ref[base + q]
                row_a = pl.multiple_of(row_a_ref[base + q], 16)
                row_b = pl.multiple_of(row_b_ref[base + q], 16)
                out_ref[q, :half, :] = product_ref[block, pl.ds(row_a, half), :]
                out_ref[q, half:, :] = product_ref[block, pl.ds(row_b, half), :]


def tiles(left, early, rights, rows, block, row_a, row_b):
    groups, width, _ = left.shape
    examples = groups * STEP
    total = sum(r.shape[0] for r in rights)
    pairs = block.shape[0]
    out = jax.ShapeDtypeStruct((pairs // 2, 2 * rows, BLOCK), f32)
    out_spec = pl.BlockSpec(out.shape, lambda i, *_: (0, 0, 0))
    return pl.pallas_call(
        functools.partial(tiles_kernel, len(rights)),
        out_shape=(out, out),
        grid_spec=pltpu.PrefetchScalarGridSpec(
            num_scalar_prefetch=3,
            grid=(examples // STEP,),
            in_specs=[pl.BlockSpec((1, width, STEP), lambda i, *_: (i, 0, 0))]
            + [pl.BlockSpec(memory_space=pl.ANY)] * (1 + len(rights)),
            out_specs=(out_spec, out_spec),
            scratch_shapes=[
                pltpu.VMEM((examples // BLOCK, early.shape[1] + total, BLOCK), f32),
                pltpu.VMEM((total, width), bf16),
                pltpu.SemaphoreType.DMA((len(rights),)),
                pltpu.SemaphoreType.DMA(()),
            ],
        ),
        compiler_params=params(32 * 2**20),
        cost_estimate=cost(total, width, examples),
    )(block, row_a, row_b, left, early, *rights)


def merge_kernel(keep_ref, got_ref, own_ref, *send_refs):
    per = own_ref.shape[0]
    own_ref[...] = keep_ref[:per] + got_ref[:per]
    for k, ref in enumerate(send_refs, 1):
        ref[...] = (keep_ref[k * per : (k + 1) * per] + got_ref[k * per : (k + 1) * per]).astype(bf16)


def merge(keep, got):
    shape = (keep.shape[0] // SIDE, *keep.shape[1:])
    return pl.pallas_call(
        merge_kernel,
        out_shape=(jax.ShapeDtypeStruct(shape, f32),)
        + (jax.ShapeDtypeStruct(shape, bf16),) * (SIDE - 1),
        compiler_params=params(32 * 2**20),
    )(keep, got)


def finish_kernel(*refs):
    ins, out_ref = refs[:-1], refs[-1]
    for k in range(out_ref.shape[0]):
        columns = []
        for at in range(0, len(ins), SIDE):
            total = ins[at][k]
            for ref in ins[at + 1 : at + SIDE]:
                total = total + ref[k].astype(f32)
            columns.append(total)
        out_ref[k] = jnp.concatenate(columns, axis=0).T


def finish(parts):
    ins = [x for part in parts for x in part]
    return pl.pallas_call(
        finish_kernel,
        out_shape=jax.ShapeDtypeStruct((ins[0].shape[0], BLOCK, BLOCK), f32),
        compiler_params=params(16 * 2**20),
    )(*ins)


def shift(array, dy, dx):
    pairs = [
        (y * SIDE + x, (y + dy) % SIDE * SIDE + (x + dx) % SIDE)
        for y in range(SIDE)
        for x in range(SIDE)
    ]
    return lax.ppermute(array, "ex", pairs)


def swap_cores(array):
    return lax.ppermute(array, "lay", [(i, i ^ 1) for i in range(2 * SIDE)])


def shift_z(array, dz):
    pairs = [(z * 2 + c, (z + dz) % SIDE * 2 + c) for z in range(SIDE) for c in range(2)]
    return lax.ppermute(array, "lay", pairs)


IN_FLIGHT = 5


class Sender:
    def __init__(self):
        self.done = []

    def __call__(self, array, dy, dx):
        if len(self.done) >= IN_FLIGHT:
            array, _ = lax.optimization_barrier((array, self.done[-IN_FLIGHT]))
        self.done.append(shift(array, dy, dx))
        return self.done[-1]


def on_device(grads, prec_in, prec_out, requests, pairs):
    grads, prec_in, prec_out = grads[0], prec_in[0], prec_out[0]
    examples, width = grads.shape
    block_count = examples // BLOCK
    blocks = grads.reshape(block_count, BLOCK, width)
    member, layer = lax.axis_index("ex"), lax.axis_index("lay")
    my_y, my_x = member // SIDE, member % SIDE
    my_z, my_core = layer // 2, layer % 2

    wanted = lax.dynamic_index_in_dim(requests, member, axis=1, keepdims=False).reshape(SIDE, SIDE)
    wanted = jnp.concatenate([wanted, wanted], 0)
    wanted = jnp.concatenate([wanted, wanted], 1)
    wanted = lax.dynamic_slice(wanted, (my_y, my_x), (SIDE, SIDE))

    send = Sender()
    need = [(0, 1), (0, 3), (1, 2), (1, 1), (1, 3), (0, 2), (0, 0), (1, 0)]
    out = []
    for row, rows in PARTS:
        listed = [
            (wanted[:, d] if f else wanted[d], row + f * rows, rows) for f, d in need
        ]
        out.append(listed)
    calls = [out[0][:3], out[0][3:6], out[0][6:] + out[1]]
    made = [v for call in calls for v in gather(blocks, call)]
    parts = []
    for p in range(len(PARTS)):
        got = dict(zip(need, made[p * len(need) : (p + 1) * len(need)]))
        for f, d in need[:6]:
            got[f, d] = send(got[f, d], 0 if f else d, d if f else 0)
        parts.append([[got[f, d] for d in range(SIDE)] for f in range(2)])
    late_in = []
    for a, b in parts:
        sides = [turn(a), turn(b)]
        got = {}
        for f, d in need[:6]:
            got[f, d] = send(sides[f][d - 1], d if f else 0, 0 if f else d)
        late_in.append(got)

    left = left_transposed(grads, prec_in, prec_out)

    own, early, late = need[6:], need[:3], need[3:6]
    order = own + early + late

    def place(f, d):
        return sum(jnp.where(d == k, at, 0) for at, (n, k) in enumerate(order) if n == f)

    first = pairs[:, 0] - member * block_count
    dy = (my_y - pairs[:, 1] // SIDE) % SIDE
    dx = (my_x - pairs[:, 1] % SIDE) % SIDE
    listed = jnp.stack([first, place(0, dx) * SIDE + dy, place(1, dy) * SIDE + dx])
    listed = listed.reshape(3, SIDE, 2, -1)
    listed = jnp.concatenate([listed, listed], 1)
    listed = lax.dynamic_slice_in_dim(listed, my_z, SIDE, 1)
    listed = jnp.where(my_core == 0, listed, listed[:, :, ::-1])
    listed = listed.transpose(0, 2, 1, 3).reshape(3, -1)

    sums = []
    for (_, rows), sides, got in zip(PARTS, parts, late_in):
        flat = {key: got[key].reshape(-1, width) for key in early + late}
        owns = [piece for f, _ in own for piece in sides[f]]
        products = early_products(left, owns, [flat[key] for key in early])
        rest = [flat[key] for key in late]
        if sums:
            *rest, _ = lax.optimization_barrier((*rest, sums[-1]))
        keep, give = tiles(left, products, rest, rows, listed[0], listed[1] * rows, listed[2] * rows)
        mine, *sends = merge(keep, swap_cores(give))
        sums.append([mine] + [shift_z(s, k) for k, s in enumerate(sends, 1)])
    return finish(sums)


def solution(mesh):
    placed = (P("lay", "ex", None), P("lay", None, None), P("lay", None, None), P(), P("ex", None))
    return jax.shard_map(
        on_device,
        mesh=mesh,
        in_specs=placed,
        out_specs=P(("ex", "lay"), None, None),
        check_vma=False,
    )
```

```python
import functools

import jax
import jax.numpy as jnp
from jax import lax
from jax.experimental import pallas as pl
from jax.experimental.pallas import tpu as pltpu
from jax.sharding import PartitionSpec as P

BLOCK = 128
SIDE = 4
PARTS = ((0, 48), (96, 16))
STEP = 256
VMEM = 60 * 2**20
bf16, f32 = jnp.bfloat16, jnp.float32
BRIEF = pl.CostEstimate(flops=1, bytes_accessed=1, transcendentals=0)


def params(limit=VMEM):
    return pltpu.CompilerParams(vmem_limit_bytes=limit)


def run_copies(copies):
    for copy in copies:
        copy.start()
    for copy in copies:
        copy.wait()


def relay(pieces, sems):
    ins = [pltpu.make_async_copy(src, mid, sems.at[0, k]) for k, (src, mid, _) in enumerate(pieces)]
    outs = [pltpu.make_async_copy(mid, dst, sems.at[1, k]) for k, (_, mid, dst) in enumerate(pieces)]
    for copy in ins:
        copy.start()
    for arrived, copy in zip(ins, outs):
        arrived.wait()
        copy.start()
    for copy in outs:
        copy.wait()


def relay_scratch(outs):
    return [pltpu.VMEM(o.shape, o.dtype) for o in outs] + [
        pltpu.SemaphoreType.DMA((2, SIDE * len(outs)))
    ]


def gather_kernel(starts, index_ref, blocks_ref, *refs):
    n = len(starts)
    outs, mids, sems = refs[:n], refs[n : 2 * n], refs[2 * n]
    pieces = []
    for at, start in enumerate(starts):
        rows = outs[at].shape[1]
        for k in range(SIDE):
            source = blocks_ref.at[index_ref[at * SIDE + k], pl.ds(start, rows)]
            pieces.append((source, mids[at].at[k], outs[at].at[k]))
    relay(pieces, sems)


def gather(blocks, bundles):
    width = blocks.shape[-1]
    outs = [jax.ShapeDtypeStruct((SIDE, rows, width), blocks.dtype) for _, _, rows in bundles]
    return pl.pallas_call(
        functools.partial(gather_kernel, [start for _, start, _ in bundles]),
        out_shape=outs,
        grid_spec=pltpu.PrefetchScalarGridSpec(
            num_scalar_prefetch=1,
            grid=(1,),
            in_specs=[pl.BlockSpec(memory_space=pl.ANY)],
            out_specs=[pl.BlockSpec(memory_space=pl.ANY)] * len(outs),
            scratch_shapes=relay_scratch(outs),
        ),
        compiler_params=params(),
        cost_estimate=BRIEF,
    )(jnp.concatenate([index for index, _, _ in bundles]), blocks)


def turn_kernel(*refs):
    n = SIDE - 1
    ins, outs, mids, sems = refs[:SIDE], refs[SIDE : SIDE + n], refs[SIDE + n : SIDE + 2 * n], refs[-1]
    pieces = [
        (ins[i].at[k + 1], mids[k].at[i], outs[k].at[i]) for k in range(n) for i in range(SIDE)
    ]
    relay(pieces, sems)


def turn(pieces):
    outs = [jax.ShapeDtypeStruct(pieces[0].shape, pieces[0].dtype)] * (SIDE - 1)
    return pl.pallas_call(
        turn_kernel,
        out_shape=outs,
        in_specs=[pl.BlockSpec(memory_space=pl.ANY)] * SIDE,
        out_specs=[pl.BlockSpec(memory_space=pl.ANY)] * (SIDE - 1),
        scratch_shapes=relay_scratch(outs),
        compiler_params=params(),
        cost_estimate=BRIEF,
    )(*pieces)


LANES = 16
OUTS = 4


def iota(shape, dim):
    return lax.broadcasted_iota(jnp.int32, shape, dim)


def one_hot(picked, shape):
    return (picked == iota(shape, 1)).astype(f32).astype(bf16)


def left_kernel(grads_ref, prec_in_ref, prec_out_ref, out_ref, inner_w_ref, outer_w_ref, inner_ref):
    rank = prec_in_ref.shape[0]
    group = rank * OUTS
    splits = rank // LANES
    per = group // splits
    width = grads_ref.shape[1]
    step = 256

    @pl.when(pl.program_id(0) == 0)
    def _():
        row = iota((group, rank), 0)
        rows = one_hot(row // per * LANES + row % LANES, (group, rank))
        columns = one_hot(row % rank, (group, rank))
        spread = lax.dot_general(
            rows, prec_in_ref[...], (((1,), (1,)), ((), ())), preferred_element_type=f32
        ).astype(bf16)
        full = lax.dot_general(spread, columns, (((1,), (1,)), ((), ())), preferred_element_type=f32)
        same = iota((group, group), 0) % per // LANES == iota((group, group), 1) // rank
        inner_w_ref[...] = jnp.where(same, full, 0.0).astype(bf16)
        columns = one_hot(iota((rank * LANES, rank), 0) // LANES, (rank * LANES, rank))
        for at in range(0, rank * LANES, step):
            rows = one_hot((iota((step, rank), 0) + at) // LANES, (step, rank))
            spread = jnp.dot(rows, prec_out_ref[...], preferred_element_type=f32).astype(bf16)
            full = lax.dot_general(spread, columns, (((1,), (1,)), ((), ())), preferred_element_type=f32)
            shape = (step, rank * LANES)
            same = iota(shape, 0) % LANES == iota(shape, 1) % LANES
            outer_w_ref[at : at + step, :] = jnp.where(same, full, 0.0).astype(bf16)

    for g in range(width // group):
        part = grads_ref[:, g * group : (g + 1) * group]
        inner = lax.dot_general(
            inner_w_ref[...], part, (((1,), (1,)), ((), ())), preferred_element_type=f32
        ).astype(bf16)
        for s in range(splits):
            inner_ref[s, g * per : (g + 1) * per, :] = inner[s * per : (s + 1) * per]
    for s in range(splits):
        for at in range(0, rank * LANES, step):
            outer = jnp.dot(
                outer_w_ref[at : at + step, :], inner_ref[s], preferred_element_type=f32
            ).astype(bf16)
            for k in range(step // LANES):
                first = (at // LANES + k) * rank + s * LANES
                out_ref[0, first : first + LANES, :] = outer[k * LANES : (k + 1) * LANES]


def left_transposed(grads, prec_in, prec_out):
    examples, width = grads.shape
    rank = prec_in.shape[-1]
    tile = STEP
    factor = pl.BlockSpec((rank, rank), lambda i: (0, 0))
    return pl.pallas_call(
        left_kernel,
        out_shape=jax.ShapeDtypeStruct((examples // tile, width, tile), bf16),
        grid=(examples // tile,),
        in_specs=[pl.BlockSpec((tile, width), lambda i: (i, 0)), factor, factor],
        out_specs=pl.BlockSpec((1, width, tile), lambda i: (i, 0, 0)),
        scratch_shapes=[
            pltpu.VMEM((rank * OUTS, rank * OUTS), bf16),
            pltpu.VMEM((rank * LANES, rank * LANES), bf16),
            pltpu.VMEM((rank // LANES, rank * LANES, tile), bf16),
        ],
        compiler_params=params(),
        cost_estimate=BRIEF,
    )(grads, prec_in, prec_out)


def fetch(rights, right_ref, sems):
    copies, at = [], 0
    for k, ref in enumerate(rights):
        rows = ref.shape[0]
        copies.append(pltpu.make_async_copy(ref, right_ref.at[pl.ds(at, rows)], sems.at[k]))
        at += rows
    run_copies(copies)


def multiply(right_ref, left_ref, product_ref, first_block, at):
    rows = right_ref.shape[0]
    product = jnp.dot(right_ref[...], left_ref[0], preferred_element_type=f32)
    for b in range(left_ref.shape[2] // BLOCK):
        product_ref[first_block + b, at : at + rows, :] = product[:, b * BLOCK : (b + 1) * BLOCK]


def early_kernel(owns, count, left_ref, *refs):
    rights, (out_ref, right_ref, sems) = refs[:count], refs[count:]
    rights = [ref.at[0] for ref in rights[:owns]] + [ref for ref in rights[owns:]]

    @pl.when(pl.program_id(0) == 0)
    def _():
        fetch(rights, right_ref, sems)

    multiply(right_ref, left_ref, out_ref, 0, 0)


def early_products(left, owns, rights):
    groups, width, _ = left.shape
    examples = groups * STEP
    rows = owns[0].shape[1]
    total = rows * len(owns) + sum(r.shape[0] for r in rights)
    owned, rights = len(owns), [*owns, *rights]
    return pl.pallas_call(
        functools.partial(early_kernel, owned, len(rights)),
        out_shape=jax.ShapeDtypeStruct((examples // BLOCK, total, BLOCK), f32),
        grid=(examples // STEP,),
        in_specs=[pl.BlockSpec((1, width, STEP), lambda i: (i, 0, 0))]
        + [pl.BlockSpec(memory_space=pl.ANY)] * len(rights),
        out_specs=pl.BlockSpec((STEP // BLOCK, total, BLOCK), lambda i: (i, 0, 0)),
        scratch_shapes=[
            pltpu.VMEM((total, width), bf16),
            pltpu.SemaphoreType.DMA((len(rights),)),
        ],
        compiler_params=params(32 * 2**20),
        cost_estimate=BRIEF,
    )(left, *rights)


def tiles_kernel(count, block_ref, row_a_ref, row_b_ref, left_ref, early_ref, *refs):
    rights = refs[:count]
    keep_ref, give_ref, product_ref, right_ref, sems, early_sem = refs[count:]
    step = pl.program_id(0)
    early = early_ref.shape[1]
    early_copy = pltpu.make_async_copy(early_ref, product_ref.at[:, pl.ds(0, early)], early_sem)

    @pl.when(step == 0)
    def _():
        early_copy.start()
        fetch(rights, right_ref, sems)

    multiply(right_ref, left_ref, product_ref, step * (left_ref.shape[2] // BLOCK), early)

    @pl.when(step == pl.num_programs(0) - 1)
    def _():
        early_copy.wait()
        half = keep_ref.shape[1] // 2
        for out_ref, base in ((give_ref, keep_ref.shape[0]), (keep_ref, 0)):
            for q in range(out_ref.shape[0]):
                block = block_ref[base + q]
                row_a = pl.multiple_of(row_a_ref[base + q], 16)
                row_b = pl.multiple_of(row_b_ref[base + q], 16)
                out_ref[q, :half, :] = product_ref[block, pl.ds(row_a, half), :]
                out_ref[q, half:, :] = product_ref[block, pl.ds(row_b, half), :]


def tiles(left, early, rights, rows, block, row_a, row_b):
    groups, width, _ = left.shape
    examples = groups * STEP
    total = sum(r.shape[0] for r in rights)
    pairs = block.shape[0]
    out = jax.ShapeDtypeStruct((pairs // 2, 2 * rows, BLOCK), f32)
    out_spec = pl.BlockSpec(out.shape, lambda i, *_: (0, 0, 0))
    return pl.pallas_call(
        functools.partial(tiles_kernel, len(rights)),
        out_shape=(out, out),
        grid_spec=pltpu.PrefetchScalarGridSpec(
            num_scalar_prefetch=3,
            grid=(examples // STEP,),
            in_specs=[pl.BlockSpec((1, width, STEP), lambda i, *_: (i, 0, 0))]
            + [pl.BlockSpec(memory_space=pl.ANY)] * (1 + len(rights)),
            out_specs=(out_spec, out_spec),
            scratch_shapes=[
                pltpu.VMEM((examples // BLOCK, early.shape[1] + total, BLOCK), f32),
                pltpu.VMEM((total, width), bf16),
                pltpu.SemaphoreType.DMA((len(rights),)),
                pltpu.SemaphoreType.DMA(()),
            ],
        ),
        compiler_params=params(32 * 2**20),
        cost_estimate=BRIEF,
    )(block, row_a, row_b, left, early, *rights)


def merge_kernel(keep_ref, got_ref, own_ref, *send_refs):
    per = own_ref.shape[0]
    own_ref[...] = keep_ref[:per] + got_ref[:per]
    for k, ref in enumerate(send_refs, 1):
        ref[...] = (keep_ref[k * per : (k + 1) * per] + got_ref[k * per : (k + 1) * per]).astype(bf16)


def merge(keep, got):
    shape = (keep.shape[0] // SIDE, *keep.shape[1:])
    return pl.pallas_call(
        merge_kernel,
        out_shape=(jax.ShapeDtypeStruct(shape, f32),)
        + (jax.ShapeDtypeStruct(shape, bf16),) * (SIDE - 1),
        compiler_params=params(32 * 2**20),
        cost_estimate=BRIEF,
    )(keep, got)


def finish_kernel(*refs):
    ins, out_ref = refs[:-1], refs[-1]
    for k in range(out_ref.shape[0]):
        columns = []
        for at in range(0, len(ins), SIDE):
            total = ins[at][k]
            for ref in ins[at + 1 : at + SIDE]:
                total = total + ref[k].astype(f32)
            columns.append(total)
        out_ref[k] = jnp.concatenate(columns, axis=0).T


def finish(parts):
    ins = [x for part in parts for x in part]
    return pl.pallas_call(
        finish_kernel,
        out_shape=jax.ShapeDtypeStruct((ins[0].shape[0], BLOCK, BLOCK), f32),
        compiler_params=params(16 * 2**20),
    )(*ins)


def shift(array, dy, dx):
    pairs = [
        (y * SIDE + x, (y + dy) % SIDE * SIDE + (x + dx) % SIDE)
        for y in range(SIDE)
        for x in range(SIDE)
    ]
    return lax.ppermute(array, "ex", pairs)


def swap_cores(array):
    return lax.ppermute(array, "lay", [(i, i ^ 1) for i in range(2 * SIDE)])


def shift_z(array, dz):
    pairs = [(z * 2 + c, (z + dz) % SIDE * 2 + c) for z in range(SIDE) for c in range(2)]
    return lax.ppermute(array, "lay", pairs)


IN_FLIGHT = 5


class Sender:
    def __init__(self):
        self.done = []

    def __call__(self, array, dy, dx):
        if len(self.done) >= IN_FLIGHT:
            array, _ = lax.optimization_barrier((array, self.done[-IN_FLIGHT]))
        arrived = shift(array, dy, dx)
        if self.done:
            arrived, _ = lax.optimization_barrier((arrived, self.done[-1]))
        self.done.append(arrived)
        return arrived


def on_device(grads, prec_in, prec_out, requests, pairs):
    grads, prec_in, prec_out = grads[0], prec_in[0], prec_out[0]
    examples, width = grads.shape
    block_count = examples // BLOCK
    blocks = grads.reshape(block_count, BLOCK, width)
    member, layer = lax.axis_index("ex"), lax.axis_index("lay")
    my_y, my_x = member // SIDE, member % SIDE
    my_z, my_core = layer // 2, layer % 2

    wanted = lax.dynamic_index_in_dim(requests, member, axis=1, keepdims=False).reshape(SIDE, SIDE)
    wanted = jnp.concatenate([wanted, wanted], 0)
    wanted = jnp.concatenate([wanted, wanted], 1)
    wanted = lax.dynamic_slice(wanted, (my_y, my_x), (SIDE, SIDE))

    send = Sender()
    need = [(0, 1), (0, 3), (1, 2), (1, 1), (1, 3), (0, 2), (0, 0), (1, 0)]
    out = []
    for row, rows in PARTS:
        listed = [
            (wanted[:, d] if f else wanted[d], row + f * rows, rows) for f, d in need
        ]
        out.append(listed)
    calls = [out[0][:3], out[0][3:6], out[0][6:] + out[1]]
    made = [v for call in calls for v in gather(blocks, call)]
    left = left_transposed(grads, prec_in, prec_out)
    parts = []
    for p in range(len(PARTS)):
        got = dict(zip(need, made[p * len(need) : (p + 1) * len(need)]))
        if p:
            got, left = lax.optimization_barrier((got, left))
        for f, d in need[:6]:
            got[f, d] = send(got[f, d], 0 if f else d, d if f else 0)
        parts.append([[got[f, d] for d in range(SIDE)] for f in range(2)])
    late_in = []
    for a, b in parts:
        sides = [turn(a), turn(b)]
        got = {}
        for f, d in need[:6]:
            got[f, d] = send(sides[f][d - 1], d if f else 0, 0 if f else d)
        late_in.append(got)

    own, early, late = need[6:], need[:3], need[3:6]
    order = own + early + late

    def place(f, d):
        return sum(jnp.where(d == k, at, 0) for at, (n, k) in enumerate(order) if n == f)

    first = pairs[:, 0] - member * block_count
    dy = (my_y - pairs[:, 1] // SIDE) % SIDE
    dx = (my_x - pairs[:, 1] % SIDE) % SIDE
    listed = jnp.stack([first, place(0, dx) * SIDE + dy, place(1, dy) * SIDE + dx])
    listed = listed.reshape(3, SIDE, 2, -1)
    listed = jnp.concatenate([listed, listed], 1)
    listed = lax.dynamic_slice_in_dim(listed, my_z, SIDE, 1)
    listed = jnp.where(my_core == 0, listed, listed[:, :, ::-1])
    listed = listed.transpose(0, 2, 1, 3).reshape(3, -1)

    sums = []
    for (_, rows), sides, got in zip(PARTS, parts, late_in):
        flat = {key: got[key].reshape(-1, width) for key in early + late}
        owns = [piece for f, _ in own for piece in sides[f]]
        products = early_products(left, owns, [flat[key] for key in early])
        rest = [flat[key] for key in late]
        if sums:
            *rest, _ = lax.optimization_barrier((*rest, sums[-1]))
        keep, give = tiles(left, products, rest, rows, listed[0], listed[1] * rows, listed[2] * rows)
        mine, *sends = merge(keep, swap_cores(give))
        sums.append([mine] + [shift_z(s, k) for k, s in enumerate(sends, 1)])
    return finish(sums)


def solution(mesh):
    placed = (P("lay", "ex", None), P("lay", None, None), P("lay", None, None), P(), P("ex", None))
    return jax.shard_map(
        on_device,
        mesh=mesh,
        in_specs=placed,
        out_specs=P(("ex", "lay"), None, None),
        check_vma=False,
    )
```

```python
import functools

import jax
import jax.numpy as jnp
from jax import lax
from jax.experimental import pallas as pl
from jax.experimental.pallas import tpu as pltpu
from jax.sharding import PartitionSpec as P

BLOCK = 128
SIDE = 4
PARTS = ((0, 64), (64, 64))
STEP = 256
VMEM = 60 * 2**20
bf16, f32 = jnp.bfloat16, jnp.float32
BRIEF = pl.CostEstimate(flops=1, bytes_accessed=1, transcendentals=0)


def params(limit=VMEM):
    return pltpu.CompilerParams(vmem_limit_bytes=limit)


def run_copies(copies):
    for copy in copies:
        copy.start()
    for copy in copies:
        copy.wait()


def relay(pieces, sems):
    ins = [pltpu.make_async_copy(src, mid, sems.at[0, k]) for k, (src, mid, _) in enumerate(pieces)]
    outs = [pltpu.make_async_copy(mid, dst, sems.at[1, k]) for k, (_, mid, dst) in enumerate(pieces)]
    for copy in ins:
        copy.start()
    for arrived, copy in zip(ins, outs):
        arrived.wait()
        copy.start()
    for copy in outs:
        copy.wait()


def relay_scratch(outs):
    return [pltpu.VMEM(o.shape, o.dtype) for o in outs] + [
        pltpu.SemaphoreType.DMA((2, SIDE * len(outs)))
    ]


def gather_kernel(starts, index_ref, blocks_ref, *refs):
    n = len(starts)
    outs, mids, sems = refs[:n], refs[n : 2 * n], refs[2 * n]
    pieces = []
    for at, start in enumerate(starts):
        rows = outs[at].shape[1]
        for k in range(SIDE):
            source = blocks_ref.at[index_ref[at * SIDE + k], pl.ds(start, rows)]
            pieces.append((source, mids[at].at[k], outs[at].at[k]))
    relay(pieces, sems)


def gather(blocks, bundles):
    width = blocks.shape[-1]
    outs = [jax.ShapeDtypeStruct((SIDE, rows, width), blocks.dtype) for _, _, rows in bundles]
    return pl.pallas_call(
        functools.partial(gather_kernel, [start for _, start, _ in bundles]),
        out_shape=outs,
        grid_spec=pltpu.PrefetchScalarGridSpec(
            num_scalar_prefetch=1,
            grid=(1,),
            in_specs=[pl.BlockSpec(memory_space=pl.ANY)],
            out_specs=[pl.BlockSpec(memory_space=pl.ANY)] * len(outs),
            scratch_shapes=relay_scratch(outs),
        ),
        compiler_params=params(),
        cost_estimate=BRIEF,
    )(jnp.concatenate([index for index, _, _ in bundles]), blocks)


def turn_kernel(*refs):
    n = SIDE - 1
    ins, outs, mids, sems = refs[:SIDE], refs[SIDE : SIDE + n], refs[SIDE + n : SIDE + 2 * n], refs[-1]
    pieces = [
        (ins[i].at[k + 1], mids[k].at[i], outs[k].at[i]) for k in range(n) for i in range(SIDE)
    ]
    relay(pieces, sems)


def turn(pieces):
    outs = [jax.ShapeDtypeStruct(pieces[0].shape, pieces[0].dtype)] * (SIDE - 1)
    return pl.pallas_call(
        turn_kernel,
        out_shape=outs,
        in_specs=[pl.BlockSpec(memory_space=pl.ANY)] * SIDE,
        out_specs=[pl.BlockSpec(memory_space=pl.ANY)] * (SIDE - 1),
        scratch_shapes=relay_scratch(outs),
        compiler_params=params(),
        cost_estimate=BRIEF,
    )(*pieces)


LANES = 16
OUTS = 4


def iota(shape, dim):
    return lax.broadcasted_iota(jnp.int32, shape, dim)


def one_hot(picked, shape):
    return (picked == iota(shape, 1)).astype(f32).astype(bf16)


def left_kernel(grads_ref, prec_in_ref, prec_out_ref, out_ref, inner_w_ref, outer_w_ref, inner_ref):
    rank = prec_in_ref.shape[0]
    group = rank * OUTS
    splits = rank // LANES
    per = group // splits
    width = grads_ref.shape[1]
    step = 256

    @pl.when(pl.program_id(0) == 0)
    def _():
        row = iota((group, rank), 0)
        rows = one_hot(row // per * LANES + row % LANES, (group, rank))
        columns = one_hot(row % rank, (group, rank))
        spread = lax.dot_general(
            rows, prec_in_ref[...], (((1,), (1,)), ((), ())), preferred_element_type=f32
        ).astype(bf16)
        full = lax.dot_general(spread, columns, (((1,), (1,)), ((), ())), preferred_element_type=f32)
        same = iota((group, group), 0) % per // LANES == iota((group, group), 1) // rank
        inner_w_ref[...] = jnp.where(same, full, 0.0).astype(bf16)
        columns = one_hot(iota((rank * LANES, rank), 0) // LANES, (rank * LANES, rank))
        for at in range(0, rank * LANES, step):
            rows = one_hot((iota((step, rank), 0) + at) // LANES, (step, rank))
            spread = jnp.dot(rows, prec_out_ref[...], preferred_element_type=f32).astype(bf16)
            full = lax.dot_general(spread, columns, (((1,), (1,)), ((), ())), preferred_element_type=f32)
            shape = (step, rank * LANES)
            same = iota(shape, 0) % LANES == iota(shape, 1) % LANES
            outer_w_ref[at : at + step, :] = jnp.where(same, full, 0.0).astype(bf16)

    for g in range(width // group):
        part = grads_ref[:, g * group : (g + 1) * group]
        inner = lax.dot_general(
            inner_w_ref[...], part, (((1,), (1,)), ((), ())), preferred_element_type=f32
        ).astype(bf16)
        for s in range(splits):
            inner_ref[s, g * per : (g + 1) * per, :] = inner[s * per : (s + 1) * per]
    for s in range(splits):
        for at in range(0, rank * LANES, step):
            outer = jnp.dot(
                outer_w_ref[at : at + step, :], inner_ref[s], preferred_element_type=f32
            ).astype(bf16)
            for k in range(step // LANES):
                first = (at // LANES + k) * rank + s * LANES
                out_ref[0, first : first + LANES, :] = outer[k * LANES : (k + 1) * LANES]


def left_transposed(grads, prec_in, prec_out):
    examples, width = grads.shape
    rank = prec_in.shape[-1]
    tile = STEP
    factor = pl.BlockSpec((rank, rank), lambda i: (0, 0))
    return pl.pallas_call(
        left_kernel,
        out_shape=jax.ShapeDtypeStruct((examples // tile, width, tile), bf16),
        grid=(examples // tile,),
        in_specs=[pl.BlockSpec((tile, width), lambda i: (i, 0)), factor, factor],
        out_specs=pl.BlockSpec((1, width, tile), lambda i: (i, 0, 0)),
        scratch_shapes=[
            pltpu.VMEM((rank * OUTS, rank * OUTS), bf16),
            pltpu.VMEM((rank * LANES, rank * LANES), bf16),
            pltpu.VMEM((rank // LANES, rank * LANES, tile), bf16),
        ],
        compiler_params=params(),
        cost_estimate=BRIEF,
    )(grads, prec_in, prec_out)


def fetch(rights, right_ref, sems):
    copies, at = [], 0
    for k, ref in enumerate(rights):
        rows = ref.shape[0]
        copies.append(pltpu.make_async_copy(ref, right_ref.at[pl.ds(at, rows)], sems.at[k]))
        at += rows
    run_copies(copies)


def multiply(right_ref, left_ref, product_ref, first_block, at):
    rows = right_ref.shape[0]
    product = jnp.dot(right_ref[...], left_ref[0], preferred_element_type=f32)
    for b in range(left_ref.shape[2] // BLOCK):
        product_ref[first_block + b, at : at + rows, :] = product[:, b * BLOCK : (b + 1) * BLOCK]


def early_kernel(count, left_ref, *refs):
    owns, (out_ref, right_ref, sems) = refs[:count], refs[count:]

    @pl.when(pl.program_id(0) == 0)
    def _():
        fetch([ref.at[0] for ref in owns], right_ref, sems)

    multiply(right_ref, left_ref, out_ref, 0, 0)


def early_products(left, owns):
    groups, width, _ = left.shape
    examples = groups * STEP
    total = sum(o.shape[1] for o in owns)
    return pl.pallas_call(
        functools.partial(early_kernel, len(owns)),
        out_shape=jax.ShapeDtypeStruct((examples // BLOCK, total, BLOCK), f32),
        grid=(groups,),
        in_specs=[pl.BlockSpec((1, width, STEP), lambda i: (i, 0, 0))]
        + [pl.BlockSpec(memory_space=pl.ANY)] * len(owns),
        out_specs=pl.BlockSpec((STEP // BLOCK, total, BLOCK), lambda i: (i, 0, 0)),
        scratch_shapes=[
            pltpu.VMEM((total, width), bf16),
            pltpu.SemaphoreType.DMA((len(owns),)),
        ],
        compiler_params=params(32 * 2**20),
        cost_estimate=BRIEF,
    )(left, *owns)


def tiles_kernel(count, block_ref, row_ref, left_ref, early_ref, *refs):
    rights = refs[:count]
    keep_ref, give_ref, product_ref, right_ref, sems, early_sem = refs[count:]
    step = pl.program_id(0)
    early = early_ref.shape[1]
    early_copy = pltpu.make_async_copy(early_ref, product_ref.at[:, pl.ds(0, early)], early_sem)

    @pl.when(step == 0)
    def _():
        early_copy.start()
        fetch(rights, right_ref, sems)

    multiply(right_ref, left_ref, product_ref, step * (left_ref.shape[2] // BLOCK), early)

    @pl.when(step == pl.num_programs(0) - 1)
    def _():
        early_copy.wait()
        rows = keep_ref.shape[1]
        for out_ref, base in ((give_ref, keep_ref.shape[0]), (keep_ref, 0)):
            for q in range(out_ref.shape[0]):
                row = pl.multiple_of(row_ref[base + q], 16)
                out_ref[q] = product_ref[block_ref[base + q], pl.ds(row, rows), :]


def tiles(left, early, rights, rows, block, row):
    groups, width, _ = left.shape
    examples = groups * STEP
    total = sum(r.shape[0] for r in rights)
    pairs = block.shape[0]
    out = jax.ShapeDtypeStruct((pairs // 2, rows, BLOCK), f32)
    out_spec = pl.BlockSpec(out.shape, lambda i, *_: (0, 0, 0))
    return pl.pallas_call(
        functools.partial(tiles_kernel, len(rights)),
        out_shape=(out, out),
        grid_spec=pltpu.PrefetchScalarGridSpec(
            num_scalar_prefetch=2,
            grid=(examples // STEP,),
            in_specs=[pl.BlockSpec((1, width, STEP), lambda i, *_: (i, 0, 0))]
            + [pl.BlockSpec(memory_space=pl.ANY)] * (1 + len(rights)),
            out_specs=(out_spec, out_spec),
            scratch_shapes=[
                pltpu.VMEM((examples // BLOCK, early.shape[1] + total, BLOCK), f32),
                pltpu.VMEM((total, width), bf16),
                pltpu.SemaphoreType.DMA((len(rights),)),
                pltpu.SemaphoreType.DMA(()),
            ],
        ),
        compiler_params=params(32 * 2**20),
        cost_estimate=BRIEF,
    )(block, row, left, early, *rights)


def merge_kernel(keep_ref, got_ref, own_ref, *send_refs):
    per = own_ref.shape[0]
    own_ref[...] = keep_ref[:per] + got_ref[:per]
    for k, ref in enumerate(send_refs, 1):
        ref[...] = (keep_ref[k * per : (k + 1) * per] + got_ref[k * per : (k + 1) * per]).astype(bf16)


def merge(keep, got):
    shape = (keep.shape[0] // SIDE, *keep.shape[1:])
    return pl.pallas_call(
        merge_kernel,
        out_shape=(jax.ShapeDtypeStruct(shape, f32),)
        + (jax.ShapeDtypeStruct(shape, bf16),) * (SIDE - 1),
        compiler_params=params(32 * 2**20),
        cost_estimate=BRIEF,
    )(keep, got)


def finish_kernel(*refs):
    ins, out_ref = refs[:-1], refs[-1]
    for k in range(out_ref.shape[0]):
        columns = []
        for at in range(0, len(ins), SIDE):
            total = ins[at][k]
            for ref in ins[at + 1 : at + SIDE]:
                total = total + ref[k].astype(f32)
            columns.append(total)
        out_ref[k] = jnp.concatenate(columns, axis=0).T


def finish(parts):
    ins = [x for part in parts for x in part]
    return pl.pallas_call(
        finish_kernel,
        out_shape=jax.ShapeDtypeStruct((ins[0].shape[0], BLOCK, BLOCK), f32),
        compiler_params=params(16 * 2**20),
    )(*ins)


def shift(array, leg, d):
    pairs = []
    for y in range(SIDE):
        for x in range(SIDE):
            for i in range(2 * SIDE):
                dy, dx = (d, 0) if leg == i % 2 else (0, d)
                to = (y + dy) % SIDE * SIDE + (x + dx) % SIDE
                pairs.append(((y * SIDE + x) * 2 * SIDE + i, to * 2 * SIDE + i))
    return lax.ppermute(array, ("ex", "lay"), pairs)


def swap_cores(array):
    return lax.ppermute(array, "lay", [(i, i ^ 1) for i in range(2 * SIDE)])


def shift_z(array, dz):
    pairs = [(z * 2 + c, (z + dz) % SIDE * 2 + c) for z in range(SIDE) for c in range(2)]
    return lax.ppermute(array, "lay", pairs)


def after(value, other):
    return lax.optimization_barrier((value, other))[0]


STEPS = (1, 3, 2)


def on_device(grads, prec_in, prec_out, requests, pairs):
    grads, prec_in, prec_out = grads[0], prec_in[0], prec_out[0]
    examples, width = grads.shape
    block_count = examples // BLOCK
    blocks = grads.reshape(block_count, BLOCK, width)
    member, layer = lax.axis_index("ex"), lax.axis_index("lay")
    my_y, my_x = member // SIDE, member % SIDE
    my_z, my_core = layer // 2, layer % 2

    wanted = lax.dynamic_index_in_dim(requests, member, axis=1, keepdims=False).reshape(SIDE, SIDE)
    wanted = jnp.concatenate([wanted, wanted], 0)
    wanted = jnp.concatenate([wanted, wanted], 1)
    wanted = lax.dynamic_slice(wanted, (my_y, my_x), (SIDE, SIDE))

    wanted = jnp.where(my_core == 0, wanted, wanted.T)

    (row1, rows1), (row2, rows2) = PARTS
    one = {}
    for d in STEPS:
        (bundle,) = gather(blocks, [(wanted[d], row1, rows1)])
        one[d] = shift(bundle, 0, d)
    one[0], *bundles = gather(
        blocks, [(wanted[0], row1, rows1)] + [(wanted[d], row2, rows2) for d in range(SIDE)]
    )
    left = left_transposed(after(grads, bundles), prec_in, prec_out)
    bundles = after(bundles, (left, one[1]))
    two = {d: shift(bundles[d], 0, d) for d in STEPS} | {0: bundles[0]}
    one = [one[d] for d in range(SIDE)]
    turned = dict(enumerate(turn(one), 1))
    one_in = [shift(turned[k], 1, k) for k in STEPS]
    early_one = early_products(after(left, turned), one)
    two = after([two[d] for d in range(SIDE)], early_one)
    turned = dict(enumerate(turn(two), 1))
    turned, early_one = lax.optimization_barrier((turned, early_one))
    early_two = early_products(left, after(two, turned))
    gate = one_in[0]
    two_in = [shift(after(turned[k], gate), 1, k) for k in STEPS]
    one_in = after(one_in, early_two)

    first = pairs[:, 0] - member * block_count
    dy = (my_y - pairs[:, 1] // SIDE) % SIDE
    dx = (my_x - pairs[:, 1] % SIDE) % SIDE
    leg0, leg1 = jnp.where(my_core == 0, dy, dx), jnp.where(my_core == 0, dx, dy)
    place = sum(jnp.where(leg1 == k, at, 0) for at, k in enumerate(STEPS, 1))
    listed = jnp.stack([first, place * SIDE + leg0])
    listed = listed.reshape(2, SIDE, 2, -1)
    listed = jnp.concatenate([listed, listed], 1)
    listed = lax.dynamic_slice_in_dim(listed, my_z, SIDE, 1)
    listed = jnp.where(my_core == 0, listed, listed[:, :, ::-1])
    listed = listed.transpose(0, 2, 1, 3).reshape(2, -1)

    sums = []
    for (_, rows), early in zip(PARTS, (early_one, early_two)):
        got = two_in if sums else one_in
        rest = [v.reshape(-1, width) for v in got]
        keep, give = tiles(left, early, rest, rows, listed[0], listed[1] * rows)
        mine, *sends = merge(keep, swap_cores(give))
        if not sums:
            sends, two_in = lax.optimization_barrier((sends, two_in))
        sums.append([mine] + [shift_z(s, k) for k, s in enumerate(sends, 1)])
    return finish(sums)


def solution(mesh):
    placed = (P("lay", "ex", None), P("lay", None, None), P("lay", None, None), P(), P("ex", None))
    return jax.shard_map(
        on_device,
        mesh=mesh,
        in_specs=placed,
        out_specs=P(("ex", "lay"), None, None),
        check_vma=False,
    )
```

```python
import functools

import jax
import jax.numpy as jnp
from jax import lax
from jax.experimental import pallas as pl
from jax.experimental.pallas import tpu as pltpu
from jax.sharding import PartitionSpec as P

BLOCK = 128
SIDE = 4
PARTS = ((0, 64), (64, 64))
STEP = 256
VMEM = 60 * 2**20
bf16, f32 = jnp.bfloat16, jnp.float32
BRIEF = pl.CostEstimate(flops=1, bytes_accessed=1, transcendentals=0)


def params(limit=VMEM):
    return pltpu.CompilerParams(vmem_limit_bytes=limit)


def run_copies(copies):
    for copy in copies:
        copy.start()
    for copy in copies:
        copy.wait()


def relay(pieces, sems):
    ins = [pltpu.make_async_copy(src, mid, sems.at[0, k]) for k, (src, mid, _) in enumerate(pieces)]
    outs = [pltpu.make_async_copy(mid, dst, sems.at[1, k]) for k, (_, mid, dst) in enumerate(pieces)]
    for copy in ins:
        copy.start()
    for arrived, copy in zip(ins, outs):
        arrived.wait()
        copy.start()
    for copy in outs:
        copy.wait()


def relay_scratch(outs):
    return [pltpu.VMEM(o.shape, o.dtype) for o in outs] + [
        pltpu.SemaphoreType.DMA((2, SIDE * len(outs)))
    ]


def gather_kernel(starts, index_ref, blocks_ref, *refs):
    n = len(starts)
    outs, mids, sems = refs[:n], refs[n : 2 * n], refs[2 * n]
    pieces = []
    for at, start in enumerate(starts):
        rows = outs[at].shape[1]
        for k in range(SIDE):
            source = blocks_ref.at[index_ref[at * SIDE + k], pl.ds(start, rows)]
            pieces.append((source, mids[at].at[k], outs[at].at[k]))
    relay(pieces, sems)


def gather(blocks, bundles):
    width = blocks.shape[-1]
    outs = [jax.ShapeDtypeStruct((SIDE, rows, width), blocks.dtype) for _, _, rows in bundles]
    return pl.pallas_call(
        functools.partial(gather_kernel, [start for _, start, _ in bundles]),
        out_shape=outs,
        grid_spec=pltpu.PrefetchScalarGridSpec(
            num_scalar_prefetch=1,
            grid=(1,),
            in_specs=[pl.BlockSpec(memory_space=pl.ANY)],
            out_specs=[pl.BlockSpec(memory_space=pl.ANY)] * len(outs),
            scratch_shapes=relay_scratch(outs),
        ),
        compiler_params=params(),
        cost_estimate=BRIEF,
    )(jnp.concatenate([index for index, _, _ in bundles]), blocks)


def turn_kernel(*refs):
    n = SIDE - 1
    ins, outs, mids, sems = refs[:SIDE], refs[SIDE : SIDE + n], refs[SIDE + n : SIDE + 2 * n], refs[-1]
    pieces = [
        (ins[i].at[k + 1], mids[k].at[i], outs[k].at[i]) for k in range(n) for i in range(SIDE)
    ]
    relay(pieces, sems)


def turn(pieces):
    outs = [jax.ShapeDtypeStruct(pieces[0].shape, pieces[0].dtype)] * (SIDE - 1)
    return pl.pallas_call(
        turn_kernel,
        out_shape=outs,
        in_specs=[pl.BlockSpec(memory_space=pl.ANY)] * SIDE,
        out_specs=[pl.BlockSpec(memory_space=pl.ANY)] * (SIDE - 1),
        scratch_shapes=relay_scratch(outs),
        compiler_params=params(),
        cost_estimate=BRIEF,
    )(*pieces)


LANES = 16
OUTS = 4


def iota(shape, dim):
    return lax.broadcasted_iota(jnp.int32, shape, dim)


def one_hot(picked, shape):
    return (picked == iota(shape, 1)).astype(f32).astype(bf16)


def left_kernel(grads_ref, prec_in_ref, prec_out_ref, out_ref, inner_w_ref, outer_w_ref, inner_ref):
    rank = prec_in_ref.shape[0]
    group = rank * OUTS
    splits = rank // LANES
    per = group // splits
    width = grads_ref.shape[1]
    step = 256

    @pl.when(pl.program_id(0) == 0)
    def _():
        row = iota((group, rank), 0)
        rows = one_hot(row // per * LANES + row % LANES, (group, rank))
        columns = one_hot(row % rank, (group, rank))
        spread = lax.dot_general(
            rows, prec_in_ref[...], (((1,), (1,)), ((), ())), preferred_element_type=f32
        ).astype(bf16)
        full = lax.dot_general(spread, columns, (((1,), (1,)), ((), ())), preferred_element_type=f32)
        same = iota((group, group), 0) % per // LANES == iota((group, group), 1) // rank
        inner_w_ref[...] = jnp.where(same, full, 0.0).astype(bf16)
        columns = one_hot(iota((rank * LANES, rank), 0) // LANES, (rank * LANES, rank))
        for at in range(0, rank * LANES, step):
            rows = one_hot((iota((step, rank), 0) + at) // LANES, (step, rank))
            spread = jnp.dot(rows, prec_out_ref[...], preferred_element_type=f32).astype(bf16)
            full = lax.dot_general(spread, columns, (((1,), (1,)), ((), ())), preferred_element_type=f32)
            shape = (step, rank * LANES)
            same = iota(shape, 0) % LANES == iota(shape, 1) % LANES
            outer_w_ref[at : at + step, :] = jnp.where(same, full, 0.0).astype(bf16)

    for g in range(width // group):
        part = grads_ref[:, g * group : (g + 1) * group]
        inner = lax.dot_general(
            inner_w_ref[...], part, (((1,), (1,)), ((), ())), preferred_element_type=f32
        ).astype(bf16)
        for s in range(splits):
            inner_ref[s, g * per : (g + 1) * per, :] = inner[s * per : (s + 1) * per]
    for s in range(splits):
        for at in range(0, rank * LANES, step):
            outer = jnp.dot(
                outer_w_ref[at : at + step, :], inner_ref[s], preferred_element_type=f32
            ).astype(bf16)
            for k in range(step // LANES):
                first = (at // LANES + k) * rank + s * LANES
                out_ref[0, first : first + LANES, :] = outer[k * LANES : (k + 1) * LANES]


def left_transposed(grads, prec_in, prec_out):
    examples, width = grads.shape
    rank = prec_in.shape[-1]
    tile = STEP
    factor = pl.BlockSpec((rank, rank), lambda i: (0, 0))
    return pl.pallas_call(
        left_kernel,
        out_shape=jax.ShapeDtypeStruct((examples // tile, width, tile), bf16),
        grid=(examples // tile,),
        in_specs=[pl.BlockSpec((tile, width), lambda i: (i, 0)), factor, factor],
        out_specs=pl.BlockSpec((1, width, tile), lambda i: (i, 0, 0)),
        scratch_shapes=[
            pltpu.VMEM((rank * OUTS, rank * OUTS), bf16),
            pltpu.VMEM((rank * LANES, rank * LANES), bf16),
            pltpu.VMEM((rank // LANES, rank * LANES, tile), bf16),
        ],
        compiler_params=params(),
        cost_estimate=BRIEF,
    )(grads, prec_in, prec_out)


def multiply(right, left_ref, product_ref, first_block, at):
    product = jnp.dot(right, left_ref[0], preferred_element_type=f32)
    for b in range(left_ref.shape[2] // BLOCK):
        columns = product[:, b * BLOCK : (b + 1) * BLOCK]
        product_ref[first_block + b, at : at + right.shape[0], :] = columns


def multiply_pieces(pieces, right_ref, sems, left_ref, product_ref, first_block, at):
    step = pl.program_id(0)

    @pl.when(step == 0)
    def _():
        copies, row = [], 0
        for k, ref in enumerate(pieces):
            slot = right_ref.at[pl.ds(row, ref.shape[0])]
            copies.append((pltpu.make_async_copy(ref, slot, sems.at[k]), row, ref.shape[0]))
            row += ref.shape[0]
        for copy, _, _ in copies:
            copy.start()
        for copy, row, rows in copies:
            copy.wait()
            multiply(right_ref[row : row + rows, :], left_ref, product_ref, first_block, at + row)

    @pl.when(step > 0)
    def _():
        multiply(right_ref[...], left_ref, product_ref, first_block, at)


def early_kernel(count, left_ref, *refs):
    owns, (out_ref, right_ref, sems) = refs[:count], refs[count:]
    multiply_pieces([ref.at[0] for ref in owns], right_ref, sems, left_ref, out_ref, 0, 0)


def early_products(left, owns):
    groups, width, _ = left.shape
    examples = groups * STEP
    total = sum(o.shape[1] for o in owns)
    return pl.pallas_call(
        functools.partial(early_kernel, len(owns)),
        out_shape=jax.ShapeDtypeStruct((examples // BLOCK, total, BLOCK), f32),
        grid=(groups,),
        in_specs=[pl.BlockSpec((1, width, STEP), lambda i: (i, 0, 0))]
        + [pl.BlockSpec(memory_space=pl.ANY)] * len(owns),
        out_specs=pl.BlockSpec((STEP // BLOCK, total, BLOCK), lambda i: (i, 0, 0)),
        scratch_shapes=[
            pltpu.VMEM((total, width), bf16),
            pltpu.SemaphoreType.DMA((len(owns),)),
        ],
        compiler_params=params(32 * 2**20),
        cost_estimate=BRIEF,
    )(left, *owns)


def tiles_kernel(count, block_ref, row_ref, left_ref, early_ref, *refs):
    rights = refs[:count]
    keep_ref, give_ref, product_ref, right_ref, sems, early_sem = refs[count:]
    step = pl.program_id(0)
    early = early_ref.shape[1]
    early_copy = pltpu.make_async_copy(early_ref, product_ref.at[:, pl.ds(0, early)], early_sem)

    @pl.when(step == 0)
    def _():
        early_copy.start()

    block = step * (left_ref.shape[2] // BLOCK)
    multiply_pieces(rights, right_ref, sems, left_ref, product_ref, block, early)

    @pl.when(step == pl.num_programs(0) - 1)
    def _():
        early_copy.wait()
        rows = keep_ref.shape[1]
        for out_ref, base in ((give_ref, keep_ref.shape[0]), (keep_ref, 0)):
            for q in range(out_ref.shape[0]):
                row = pl.multiple_of(row_ref[base + q], 16)
                out_ref[q] = product_ref[block_ref[base + q], pl.ds(row, rows), :]


def tiles(left, early, rights, rows, block, row):
    groups, width, _ = left.shape
    examples = groups * STEP
    total = sum(r.shape[0] for r in rights)
    pairs = block.shape[0]
    out = jax.ShapeDtypeStruct((pairs // 2, rows, BLOCK), f32)
    out_spec = pl.BlockSpec(out.shape, lambda i, *_: (0, 0, 0))
    return pl.pallas_call(
        functools.partial(tiles_kernel, len(rights)),
        out_shape=(out, out),
        grid_spec=pltpu.PrefetchScalarGridSpec(
            num_scalar_prefetch=2,
            grid=(examples // STEP,),
            in_specs=[pl.BlockSpec((1, width, STEP), lambda i, *_: (i, 0, 0))]
            + [pl.BlockSpec(memory_space=pl.ANY)] * (1 + len(rights)),
            out_specs=(out_spec, out_spec),
            scratch_shapes=[
                pltpu.VMEM((examples // BLOCK, early.shape[1] + total, BLOCK), f32),
                pltpu.VMEM((total, width), bf16),
                pltpu.SemaphoreType.DMA((len(rights),)),
                pltpu.SemaphoreType.DMA(()),
            ],
        ),
        compiler_params=params(32 * 2**20),
        cost_estimate=BRIEF,
    )(block, row, left, early, *rights)


def merge_kernel(keep_ref, got_ref, own_ref, *send_refs):
    per = own_ref.shape[0]
    own_ref[...] = keep_ref[:per] + got_ref[:per]
    for k, ref in enumerate(send_refs, 1):
        ref[...] = (keep_ref[k * per : (k + 1) * per] + got_ref[k * per : (k + 1) * per]).astype(bf16)


def merge(keep, got):
    shape = (keep.shape[0] // SIDE, *keep.shape[1:])
    return pl.pallas_call(
        merge_kernel,
        out_shape=(jax.ShapeDtypeStruct(shape, f32),)
        + (jax.ShapeDtypeStruct(shape, bf16),) * (SIDE - 1),
        compiler_params=params(32 * 2**20),
        cost_estimate=BRIEF,
    )(keep, got)


def finish_kernel(*refs):
    ins, out_ref = refs[:-1], refs[-1]
    for k in range(out_ref.shape[0]):
        columns = []
        for at in range(0, len(ins), SIDE):
            total = ins[at][k]
            for ref in ins[at + 1 : at + SIDE]:
                total = total + ref[k].astype(f32)
            columns.append(total)
        out_ref[k] = jnp.concatenate(columns, axis=0).T


def finish(parts):
    ins = [x for part in parts for x in part]
    return pl.pallas_call(
        finish_kernel,
        out_shape=jax.ShapeDtypeStruct((ins[0].shape[0], BLOCK, BLOCK), f32),
        compiler_params=params(16 * 2**20),
    )(*ins)


def shift(array, leg, d):
    pairs = []
    for y in range(SIDE):
        for x in range(SIDE):
            for i in range(2 * SIDE):
                dy, dx = (d, 0) if leg == i % 2 else (0, d)
                to = (y + dy) % SIDE * SIDE + (x + dx) % SIDE
                pairs.append(((y * SIDE + x) * 2 * SIDE + i, to * 2 * SIDE + i))
    return lax.ppermute(array, ("ex", "lay"), pairs)


def swap_cores(array):
    return lax.ppermute(array, "lay", [(i, i ^ 1) for i in range(2 * SIDE)])


def shift_z(array, dz):
    pairs = [(z * 2 + c, (z + dz) % SIDE * 2 + c) for z in range(SIDE) for c in range(2)]
    return lax.ppermute(array, "lay", pairs)


def after(value, other):
    return lax.optimization_barrier((value, other))[0]


STEPS = (1, 3, 2)


def on_device(grads, prec_in, prec_out, requests, pairs):
    grads, prec_in, prec_out = grads[0], prec_in[0], prec_out[0]
    examples, width = grads.shape
    block_count = examples // BLOCK
    blocks = grads.reshape(block_count, BLOCK, width)
    member, layer = lax.axis_index("ex"), lax.axis_index("lay")
    my_y, my_x = member // SIDE, member % SIDE
    my_z, my_core = layer // 2, layer % 2

    wanted = lax.dynamic_index_in_dim(requests, member, axis=1, keepdims=False).reshape(SIDE, SIDE)
    wanted = jnp.concatenate([wanted, wanted], 0)
    wanted = jnp.concatenate([wanted, wanted], 1)
    wanted = lax.dynamic_slice(wanted, (my_y, my_x), (SIDE, SIDE))

    wanted = jnp.where(my_core == 0, wanted, wanted.T)

    (row1, rows1), (row2, rows2) = PARTS
    one = {}
    for d in STEPS:
        (bundle,) = gather(blocks, [(wanted[d], row1, rows1)])
        one[d] = shift(bundle, 0, d)
    one[0], *bundles = gather(
        blocks, [(wanted[0], row1, rows1)] + [(wanted[d], row2, rows2) for d in range(SIDE)]
    )
    left = left_transposed(after(grads, bundles), prec_in, prec_out)
    bundles = after(bundles, (left, one[1]))
    two = {d: shift(bundles[d], 0, d) for d in STEPS} | {0: bundles[0]}
    one = [one[d] for d in range(SIDE)]
    turned = dict(enumerate(turn(one), 1))
    one_in = [shift(turned[k], 1, k) for k in STEPS]
    early_one = early_products(after(left, turned), one)
    two = after([two[d] for d in range(SIDE)], early_one)
    turned = dict(enumerate(turn(two), 1))
    turned, early_one = lax.optimization_barrier((turned, early_one))
    early_two = early_products(left, after(two, turned))
    gate = one_in[0]
    two_in = [shift(after(turned[k], gate), 1, k) for k in STEPS]
    one_in = after(one_in, early_two)

    first = pairs[:, 0] - member * block_count
    dy = (my_y - pairs[:, 1] // SIDE) % SIDE
    dx = (my_x - pairs[:, 1] % SIDE) % SIDE
    leg0, leg1 = jnp.where(my_core == 0, dy, dx), jnp.where(my_core == 0, dx, dy)
    place = sum(jnp.where(leg1 == k, at, 0) for at, k in enumerate(STEPS, 1))
    listed = jnp.stack([first, place * SIDE + leg0])
    listed = listed.reshape(2, SIDE, 2, -1)
    listed = jnp.concatenate([listed, listed], 1)
    listed = lax.dynamic_slice_in_dim(listed, my_z, SIDE, 1)
    listed = jnp.where(my_core == 0, listed, listed[:, :, ::-1])
    listed = listed.transpose(0, 2, 1, 3).reshape(2, -1)

    sums = []
    for (_, rows), early in zip(PARTS, (early_one, early_two)):
        got = two_in if sums else one_in
        rest = [v.reshape(-1, width) for v in got]
        if sums:
            rest = after(rest, sums[-1])
        keep, give = tiles(left, early, rest, rows, listed[0], listed[1] * rows)
        mine, *sends = merge(keep, swap_cores(give))
        sums.append([mine] + [shift_z(s, k) for k, s in enumerate(sends, 1)])
    return finish(sums)


def solution(mesh):
    placed = (P("lay", "ex", None), P("lay", None, None), P("lay", None, None), P(), P("ex", None))
    return jax.shard_map(
        on_device,
        mesh=mesh,
        in_specs=placed,
        out_specs=P(("ex", "lay"), None, None),
        check_vma=False,
    )
```

```python
import functools

import jax
import jax.numpy as jnp
from jax import lax
from jax.experimental import pallas as pl
from jax.experimental.pallas import tpu as pltpu
from jax.sharding import PartitionSpec as P

BLOCK = 128
SIDE = 4
PARTS = ((0, 64), (64, 64))
STEP = 256
VMEM = 60 * 2**20
bf16, f32 = jnp.bfloat16, jnp.float32
BRIEF = pl.CostEstimate(flops=1, bytes_accessed=1, transcendentals=0)


def params(limit=VMEM):
    return pltpu.CompilerParams(vmem_limit_bytes=limit)


def run_copies(copies):
    for copy in copies:
        copy.start()
    for copy in copies:
        copy.wait()


def relay(pieces, sems):
    ins = [pltpu.make_async_copy(src, mid, sems.at[0, k]) for k, (src, mid, _) in enumerate(pieces)]
    outs = [pltpu.make_async_copy(mid, dst, sems.at[1, k]) for k, (_, mid, dst) in enumerate(pieces)]
    for copy in ins:
        copy.start()
    for arrived, copy in zip(ins, outs):
        arrived.wait()
        copy.start()
    for copy in outs:
        copy.wait()


def relay_scratch(outs):
    return [pltpu.VMEM(o.shape, o.dtype) for o in outs] + [
        pltpu.SemaphoreType.DMA((2, SIDE * len(outs)))
    ]


def gather_kernel(starts, index_ref, blocks_ref, *refs):
    n = len(starts)
    outs, mids, sems = refs[:n], refs[n : 2 * n], refs[2 * n]
    pieces = []
    for at, start in enumerate(starts):
        rows = outs[at].shape[1]
        for k in range(SIDE):
            source = blocks_ref.at[index_ref[at * SIDE + k], pl.ds(start, rows)]
            pieces.append((source, mids[at].at[k], outs[at].at[k]))
    relay(pieces, sems)


def gather(blocks, bundles):
    width = blocks.shape[-1]
    outs = [jax.ShapeDtypeStruct((SIDE, rows, width), blocks.dtype) for _, _, rows in bundles]
    return pl.pallas_call(
        functools.partial(gather_kernel, [start for _, start, _ in bundles]),
        out_shape=outs,
        grid_spec=pltpu.PrefetchScalarGridSpec(
            num_scalar_prefetch=1,
            grid=(1,),
            in_specs=[pl.BlockSpec(memory_space=pl.ANY)],
            out_specs=[pl.BlockSpec(memory_space=pl.ANY)] * len(outs),
            scratch_shapes=relay_scratch(outs),
        ),
        compiler_params=params(),
        cost_estimate=BRIEF,
    )(jnp.concatenate([index for index, _, _ in bundles]), blocks)


def turn_kernel(*refs):
    n = SIDE - 1
    ins, outs, mids, sems = refs[:SIDE], refs[SIDE : SIDE + n], refs[SIDE + n : SIDE + 2 * n], refs[-1]
    pieces = [
        (ins[i].at[k + 1], mids[k].at[i], outs[k].at[i]) for k in range(n) for i in range(SIDE)
    ]
    relay(pieces, sems)


def turn(pieces):
    outs = [jax.ShapeDtypeStruct(pieces[0].shape, pieces[0].dtype)] * (SIDE - 1)
    return pl.pallas_call(
        turn_kernel,
        out_shape=outs,
        in_specs=[pl.BlockSpec(memory_space=pl.ANY)] * SIDE,
        out_specs=[pl.BlockSpec(memory_space=pl.ANY)] * (SIDE - 1),
        scratch_shapes=relay_scratch(outs),
        compiler_params=params(),
        cost_estimate=BRIEF,
    )(*pieces)


LANES = 16
OUTS = 4


def iota(shape, dim):
    return lax.broadcasted_iota(jnp.int32, shape, dim)


def one_hot(picked, shape):
    return (picked == iota(shape, 1)).astype(f32).astype(bf16)


def left_kernel(grads_ref, prec_in_ref, prec_out_ref, out_ref, inner_w_ref, outer_w_ref, inner_ref):
    rank = prec_in_ref.shape[0]
    group = rank * OUTS
    splits = rank // LANES
    per = group // splits
    width = grads_ref.shape[1]
    step = 256

    @pl.when(pl.program_id(0) == 0)
    def _():
        row = iota((group, rank), 0)
        rows = one_hot(row // per * LANES + row % LANES, (group, rank))
        columns = one_hot(row % rank, (group, rank))
        spread = lax.dot_general(
            rows, prec_in_ref[...], (((1,), (1,)), ((), ())), preferred_element_type=f32
        ).astype(bf16)
        full = lax.dot_general(spread, columns, (((1,), (1,)), ((), ())), preferred_element_type=f32)
        same = iota((group, group), 0) % per // LANES == iota((group, group), 1) // rank
        inner_w_ref[...] = jnp.where(same, full, 0.0).astype(bf16)
        columns = one_hot(iota((rank * LANES, rank), 0) // LANES, (rank * LANES, rank))
        for at in range(0, rank * LANES, step):
            rows = one_hot((iota((step, rank), 0) + at) // LANES, (step, rank))
            spread = jnp.dot(rows, prec_out_ref[...], preferred_element_type=f32).astype(bf16)
            full = lax.dot_general(spread, columns, (((1,), (1,)), ((), ())), preferred_element_type=f32)
            shape = (step, rank * LANES)
            same = iota(shape, 0) % LANES == iota(shape, 1) % LANES
            outer_w_ref[at : at + step, :] = jnp.where(same, full, 0.0).astype(bf16)

    for g in range(width // group):
        part = grads_ref[:, g * group : (g + 1) * group]
        inner = lax.dot_general(
            inner_w_ref[...], part, (((1,), (1,)), ((), ())), preferred_element_type=f32
        ).astype(bf16)
        for s in range(splits):
            inner_ref[s, g * per : (g + 1) * per, :] = inner[s * per : (s + 1) * per]
    for s in range(splits):
        for at in range(0, rank * LANES, step):
            outer = jnp.dot(
                outer_w_ref[at : at + step, :], inner_ref[s], preferred_element_type=f32
            ).astype(bf16)
            for k in range(step // LANES):
                first = (at // LANES + k) * rank + s * LANES
                out_ref[0, first : first + LANES, :] = outer[k * LANES : (k + 1) * LANES]


def left_transposed(grads, prec_in, prec_out):
    examples, width = grads.shape
    rank = prec_in.shape[-1]
    tile = STEP
    factor = pl.BlockSpec((rank, rank), lambda i: (0, 0))
    return pl.pallas_call(
        left_kernel,
        out_shape=jax.ShapeDtypeStruct((examples // tile, width, tile), bf16),
        grid=(examples // tile,),
        in_specs=[pl.BlockSpec((tile, width), lambda i: (i, 0)), factor, factor],
        out_specs=pl.BlockSpec((1, width, tile), lambda i: (i, 0, 0)),
        scratch_shapes=[
            pltpu.VMEM((rank * OUTS, rank * OUTS), bf16),
            pltpu.VMEM((rank * LANES, rank * LANES), bf16),
            pltpu.VMEM((rank // LANES, rank * LANES, tile), bf16),
        ],
        compiler_params=params(),
        cost_estimate=BRIEF,
    )(grads, prec_in, prec_out)


def multiply(right, left_ref, product_ref, first_block, at):
    product = jnp.dot(right, left_ref[0], preferred_element_type=f32)
    for b in range(left_ref.shape[2] // BLOCK):
        columns = product[:, b * BLOCK : (b + 1) * BLOCK]
        product_ref[first_block + b, at : at + right.shape[0], :] = columns


def multiply_pieces(pieces, right_ref, sems, left_ref, product_ref, first_block, at):
    step = pl.program_id(0)

    @pl.when(step == 0)
    def _():
        copies, row = [], 0
        for k, ref in enumerate(pieces):
            slot = right_ref.at[pl.ds(row, ref.shape[0])]
            copies.append((pltpu.make_async_copy(ref, slot, sems.at[k]), row, ref.shape[0]))
            row += ref.shape[0]
        for copy, _, _ in copies:
            copy.start()
        for copy, row, rows in copies:
            copy.wait()
            multiply(right_ref[row : row + rows, :], left_ref, product_ref, first_block, at + row)

    @pl.when(step > 0)
    def _():
        multiply(right_ref[...], left_ref, product_ref, first_block, at)


def early_kernel(count, left_ref, *refs):
    owns, (out_ref, right_ref, sems) = refs[:count], refs[count:]
    multiply_pieces([ref.at[0] for ref in owns], right_ref, sems, left_ref, out_ref, 0, 0)


def early_products(left, owns):
    groups, width, _ = left.shape
    examples = groups * STEP
    total = sum(o.shape[1] for o in owns)
    return pl.pallas_call(
        functools.partial(early_kernel, len(owns)),
        out_shape=jax.ShapeDtypeStruct((examples // BLOCK, total, BLOCK), f32),
        grid=(groups,),
        in_specs=[pl.BlockSpec((1, width, STEP), lambda i: (i, 0, 0))]
        + [pl.BlockSpec(memory_space=pl.ANY)] * len(owns),
        out_specs=pl.BlockSpec((STEP // BLOCK, total, BLOCK), lambda i: (i, 0, 0)),
        scratch_shapes=[
            pltpu.VMEM((total, width), bf16),
            pltpu.SemaphoreType.DMA((len(owns),)),
        ],
        compiler_params=params(32 * 2**20),
        cost_estimate=BRIEF,
    )(left, *owns)


def tiles_kernel(count, block_ref, row_ref, left_ref, early_ref, *refs):
    rights = refs[:count]
    keep_ref, give_ref, product_ref, right_ref, sems, early_sem = refs[count:]
    step = pl.program_id(0)
    early = early_ref.shape[1]
    early_copy = pltpu.make_async_copy(early_ref, product_ref.at[:, pl.ds(0, early)], early_sem)

    @pl.when(step == 0)
    def _():
        early_copy.start()

    block = step * (left_ref.shape[2] // BLOCK)
    multiply_pieces(rights, right_ref, sems, left_ref, product_ref, block, early)

    @pl.when(step == pl.num_programs(0) - 1)
    def _():
        early_copy.wait()
        rows = keep_ref.shape[1]
        for out_ref, base in ((give_ref, keep_ref.shape[0]), (keep_ref, 0)):
            for q in range(out_ref.shape[0]):
                row = pl.multiple_of(row_ref[base + q], 16)
                out_ref[q] = product_ref[block_ref[base + q], pl.ds(row, rows), :]


def tiles(left, early, rights, rows, block, row):
    groups, width, _ = left.shape
    examples = groups * STEP
    total = sum(r.shape[0] for r in rights)
    pairs = block.shape[0]
    out = jax.ShapeDtypeStruct((pairs // 2, rows, BLOCK), f32)
    out_spec = pl.BlockSpec(out.shape, lambda i, *_: (0, 0, 0))
    return pl.pallas_call(
        functools.partial(tiles_kernel, len(rights)),
        out_shape=(out, out),
        grid_spec=pltpu.PrefetchScalarGridSpec(
            num_scalar_prefetch=2,
            grid=(examples // STEP,),
            in_specs=[pl.BlockSpec((1, width, STEP), lambda i, *_: (i, 0, 0))]
            + [pl.BlockSpec(memory_space=pl.ANY)] * (1 + len(rights)),
            out_specs=(out_spec, out_spec),
            scratch_shapes=[
                pltpu.VMEM((examples // BLOCK, early.shape[1] + total, BLOCK), f32),
                pltpu.VMEM((total, width), bf16),
                pltpu.SemaphoreType.DMA((len(rights),)),
                pltpu.SemaphoreType.DMA(()),
            ],
        ),
        compiler_params=params(32 * 2**20),
        cost_estimate=BRIEF,
    )(block, row, left, early, *rights)


def merge_kernel(keep_ref, got_ref, own_ref, *send_refs):
    per = own_ref.shape[0]
    own_ref[...] = keep_ref[:per] + got_ref[:per]
    for k, ref in enumerate(send_refs, 1):
        ref[...] = (keep_ref[k * per : (k + 1) * per] + got_ref[k * per : (k + 1) * per]).astype(bf16)


def merge(keep, got):
    shape = (keep.shape[0] // SIDE, *keep.shape[1:])
    return pl.pallas_call(
        merge_kernel,
        out_shape=(jax.ShapeDtypeStruct(shape, f32),)
        + (jax.ShapeDtypeStruct(shape, bf16),) * (SIDE - 1),
        compiler_params=params(32 * 2**20),
        cost_estimate=BRIEF,
    )(keep, got)


def finish_kernel(*refs):
    ins, out_ref = refs[:-1], refs[-1]
    for k in range(out_ref.shape[0]):
        columns = []
        for at in range(0, len(ins), SIDE):
            total = ins[at][k]
            for ref in ins[at + 1 : at + SIDE]:
                total = total + ref[k].astype(f32)
            columns.append(total)
        out_ref[k] = jnp.concatenate(columns, axis=0).T


def finish(parts):
    ins = [x for part in parts for x in part]
    return pl.pallas_call(
        finish_kernel,
        out_shape=jax.ShapeDtypeStruct((ins[0].shape[0], BLOCK, BLOCK), f32),
        compiler_params=params(16 * 2**20),
    )(*ins)


def shift(array, leg, d):
    pairs = []
    for y in range(SIDE):
        for x in range(SIDE):
            for i in range(2 * SIDE):
                dy, dx = (d, 0) if leg == i % 2 else (0, d)
                to = (y + dy) % SIDE * SIDE + (x + dx) % SIDE
                pairs.append(((y * SIDE + x) * 2 * SIDE + i, to * 2 * SIDE + i))
    return lax.ppermute(array, ("ex", "lay"), pairs)


def swap_cores(array):
    return lax.ppermute(array, "lay", [(i, i ^ 1) for i in range(2 * SIDE)])


def shift_z(array, dz):
    pairs = [(z * 2 + c, (z + dz) % SIDE * 2 + c) for z in range(SIDE) for c in range(2)]
    return lax.ppermute(array, "lay", pairs)


def after(value, other):
    return lax.optimization_barrier((value, other))[0]


STEPS = (1, 3, 2)


def on_device(grads, prec_in, prec_out, requests, pairs):
    grads, prec_in, prec_out = grads[0], prec_in[0], prec_out[0]
    examples, width = grads.shape
    block_count = examples // BLOCK
    blocks = grads.reshape(block_count, BLOCK, width)
    member, layer = lax.axis_index("ex"), lax.axis_index("lay")
    my_y, my_x = member // SIDE, member % SIDE
    my_z, my_core = layer // 2, layer % 2

    wanted = lax.dynamic_index_in_dim(requests, member, axis=1, keepdims=False).reshape(SIDE, SIDE)
    wanted = jnp.concatenate([wanted, wanted], 0)
    wanted = jnp.concatenate([wanted, wanted], 1)
    wanted = lax.dynamic_slice(wanted, (my_y, my_x), (SIDE, SIDE))

    wanted = jnp.where(my_core == 0, wanted, wanted.T)

    (row1, rows1), (row2, rows2) = PARTS
    one = {}
    for d in STEPS:
        (bundle,) = gather(blocks, [(wanted[d], row1, rows1)])
        one[d] = shift(bundle, 0, d)
    one[0], *bundles = gather(
        blocks, [(wanted[0], row1, rows1)] + [(wanted[d], row2, rows2) for d in range(SIDE)]
    )
    left = left_transposed(after(grads, bundles), prec_in, prec_out)
    bundles = after(bundles, (left, one[1]))
    two = {d: shift(bundles[d], 0, d) for d in STEPS} | {0: bundles[0]}
    one = [one[d] for d in range(SIDE)]
    turned = dict(enumerate(turn(one), 1))
    one_in = [shift(after(turned[k], two[1]), 1, k) for k in STEPS]
    early_one = early_products(after(left, turned), one)
    two = after([two[d] for d in range(SIDE)], early_one)
    turned = dict(enumerate(turn(two), 1))
    turned, early_one = lax.optimization_barrier((turned, early_one))
    early_two = early_products(left, after(two, turned))
    gate = one_in[0]
    two_in = [shift(after(turned[k], gate), 1, k) for k in STEPS]
    one_in = after(one_in, early_two)

    first = pairs[:, 0] - member * block_count
    dy = (my_y - pairs[:, 1] // SIDE) % SIDE
    dx = (my_x - pairs[:, 1] % SIDE) % SIDE
    leg0, leg1 = jnp.where(my_core == 0, dy, dx), jnp.where(my_core == 0, dx, dy)
    place = sum(jnp.where(leg1 == k, at, 0) for at, k in enumerate(STEPS, 1))
    listed = jnp.stack([first, place * SIDE + leg0])
    listed = listed.reshape(2, SIDE, 2, -1)
    listed = jnp.concatenate([listed, listed], 1)
    listed = lax.dynamic_slice_in_dim(listed, my_z, SIDE, 1)
    listed = jnp.where(my_core == 0, listed, listed[:, :, ::-1])
    listed = listed.transpose(0, 2, 1, 3).reshape(2, -1)

    sums = []
    for (_, rows), early in zip(PARTS, (early_one, early_two)):
        got = two_in if sums else one_in
        rest = [v.reshape(-1, width) for v in got]
        if sums:
            rest = after(rest, sums[-1])
        keep, give = tiles(left, early, rest, rows, listed[0], listed[1] * rows)
        mine, *sends = merge(keep, swap_cores(give))
        sums.append([mine] + [shift_z(s, k) for k, s in enumerate(sends, 1)])
    return finish(sums)


def solution(mesh):
    placed = (P("lay", "ex", None), P("lay", None, None), P("lay", None, None), P(), P("ex", None))
    return jax.shard_map(
        on_device,
        mesh=mesh,
        in_specs=placed,
        out_specs=P(("ex", "lay"), None, None),
        check_vma=False,
    )
```

```python
import functools

import jax
import jax.numpy as jnp
from jax import lax
from jax.experimental import pallas as pl
from jax.experimental.pallas import tpu as pltpu
from jax.sharding import PartitionSpec as P

BLOCK = 128
SIDE = 4
PARTS = ((0, 64), (64, 64))
STEP = 512
VMEM = 60 * 2**20
bf16, f32 = jnp.bfloat16, jnp.float32
BRIEF = pl.CostEstimate(flops=1, bytes_accessed=1, transcendentals=0)


def params(limit=VMEM):
    return pltpu.CompilerParams(vmem_limit_bytes=limit)


def run_copies(copies):
    for copy in copies:
        copy.start()
    for copy in copies:
        copy.wait()


def relay(pieces, sems):
    ins = [pltpu.make_async_copy(src, mid, sems.at[0, k]) for k, (src, mid, _) in enumerate(pieces)]
    outs = [pltpu.make_async_copy(mid, dst, sems.at[1, k]) for k, (_, mid, dst) in enumerate(pieces)]
    for copy in ins:
        copy.start()
    for arrived, copy in zip(ins, outs):
        arrived.wait()
        copy.start()
    for copy in outs:
        copy.wait()


def relay_scratch(outs):
    return [pltpu.VMEM(o.shape, o.dtype) for o in outs] + [
        pltpu.SemaphoreType.DMA((2, SIDE * len(outs)))
    ]


def gather_kernel(starts, index_ref, blocks_ref, *refs):
    n = len(starts)
    outs, mids, sems = refs[:n], refs[n : 2 * n], refs[2 * n]
    pieces = []
    for at, start in enumerate(starts):
        rows = outs[at].shape[1]
        for k in range(SIDE):
            source = blocks_ref.at[index_ref[at * SIDE + k], pl.ds(start, rows)]
            pieces.append((source, mids[at].at[k], outs[at].at[k]))
    relay(pieces, sems)


def gather(blocks, bundles):
    width = blocks.shape[-1]
    outs = [jax.ShapeDtypeStruct((SIDE, rows, width), blocks.dtype) for _, _, rows in bundles]
    return pl.pallas_call(
        functools.partial(gather_kernel, [start for _, start, _ in bundles]),
        out_shape=outs,
        grid_spec=pltpu.PrefetchScalarGridSpec(
            num_scalar_prefetch=1,
            grid=(1,),
            in_specs=[pl.BlockSpec(memory_space=pl.ANY)],
            out_specs=[pl.BlockSpec(memory_space=pl.ANY)] * len(outs),
            scratch_shapes=relay_scratch(outs),
        ),
        compiler_params=params(),
        cost_estimate=BRIEF,
    )(jnp.concatenate([index for index, _, _ in bundles]), blocks)


def turn_kernel(*refs):
    n = SIDE - 1
    ins, outs, mids, sems = refs[:SIDE], refs[SIDE : SIDE + n], refs[SIDE + n : SIDE + 2 * n], refs[-1]
    pieces = [
        (ins[i].at[k + 1], mids[k].at[i], outs[k].at[i]) for k in range(n) for i in range(SIDE)
    ]
    relay(pieces, sems)


def turn(pieces):
    outs = [jax.ShapeDtypeStruct(pieces[0].shape, pieces[0].dtype)] * (SIDE - 1)
    return pl.pallas_call(
        turn_kernel,
        out_shape=outs,
        in_specs=[pl.BlockSpec(memory_space=pl.ANY)] * SIDE,
        out_specs=[pl.BlockSpec(memory_space=pl.ANY)] * (SIDE - 1),
        scratch_shapes=relay_scratch(outs),
        compiler_params=params(),
        cost_estimate=BRIEF,
    )(*pieces)


LANES = 16
OUTS = 4


def iota(shape, dim):
    return lax.broadcasted_iota(jnp.int32, shape, dim)


def one_hot(picked, shape):
    return (picked == iota(shape, 1)).astype(f32).astype(bf16)


def left_kernel(grads_ref, prec_in_ref, prec_out_ref, out_ref, inner_w_ref, outer_w_ref, inner_ref):
    rank = prec_in_ref.shape[0]
    group = rank * OUTS
    splits = rank // LANES
    per = group // splits
    width = grads_ref.shape[1]
    step = 256

    @pl.when(pl.program_id(0) == 0)
    def _():
        row = iota((group, rank), 0)
        rows = one_hot(row // per * LANES + row % LANES, (group, rank))
        columns = one_hot(row % rank, (group, rank))
        spread = lax.dot_general(
            rows, prec_in_ref[...], (((1,), (1,)), ((), ())), preferred_element_type=f32
        ).astype(bf16)
        full = lax.dot_general(spread, columns, (((1,), (1,)), ((), ())), preferred_element_type=f32)
        same = iota((group, group), 0) % per // LANES == iota((group, group), 1) // rank
        inner_w_ref[...] = jnp.where(same, full, 0.0).astype(bf16)
        columns = one_hot(iota((rank * LANES, rank), 0) // LANES, (rank * LANES, rank))
        for at in range(0, rank * LANES, step):
            rows = one_hot((iota((step, rank), 0) + at) // LANES, (step, rank))
            spread = jnp.dot(rows, prec_out_ref[...], preferred_element_type=f32).astype(bf16)
            full = lax.dot_general(spread, columns, (((1,), (1,)), ((), ())), preferred_element_type=f32)
            shape = (step, rank * LANES)
            same = iota(shape, 0) % LANES == iota(shape, 1) % LANES
            outer_w_ref[at : at + step, :] = jnp.where(same, full, 0.0).astype(bf16)

    for g in range(width // group):
        part = grads_ref[:, g * group : (g + 1) * group]
        inner = lax.dot_general(
            inner_w_ref[...], part, (((1,), (1,)), ((), ())), preferred_element_type=f32
        ).astype(bf16)
        for s in range(splits):
            inner_ref[s, g * per : (g + 1) * per, :] = inner[s * per : (s + 1) * per]
    for s in range(splits):
        for at in range(0, rank * LANES, step):
            outer = jnp.dot(
                outer_w_ref[at : at + step, :], inner_ref[s], preferred_element_type=f32
            ).astype(bf16)
            for k in range(step // LANES):
                first = (at // LANES + k) * rank + s * LANES
                out_ref[0, first : first + LANES, :] = outer[k * LANES : (k + 1) * LANES]


def left_transposed(grads, prec_in, prec_out):
    examples, width = grads.shape
    rank = prec_in.shape[-1]
    tile = STEP
    factor = pl.BlockSpec((rank, rank), lambda i: (0, 0))
    return pl.pallas_call(
        left_kernel,
        out_shape=jax.ShapeDtypeStruct((examples // tile, width, tile), bf16),
        grid=(examples // tile,),
        in_specs=[pl.BlockSpec((tile, width), lambda i: (i, 0)), factor, factor],
        out_specs=pl.BlockSpec((1, width, tile), lambda i: (i, 0, 0)),
        scratch_shapes=[
            pltpu.VMEM((rank * OUTS, rank * OUTS), bf16),
            pltpu.VMEM((rank * LANES, rank * LANES), bf16),
            pltpu.VMEM((rank // LANES, rank * LANES, tile), bf16),
        ],
        compiler_params=params(),
        cost_estimate=BRIEF,
    )(grads, prec_in, prec_out)


def multiply(right, left_ref, product_ref, first_block, at):
    product = jnp.dot(right, left_ref[0], preferred_element_type=f32)
    for b in range(left_ref.shape[2] // BLOCK):
        columns = product[:, b * BLOCK : (b + 1) * BLOCK]
        product_ref[first_block + b, at : at + right.shape[0], :] = columns


def multiply_pieces(pieces, right_ref, sems, left_ref, product_ref, first_block, at):
    step = pl.program_id(0)

    @pl.when(step == 0)
    def _():
        copies, row = [], 0
        for k, ref in enumerate(pieces):
            slot = right_ref.at[pl.ds(row, ref.shape[0])]
            copies.append((pltpu.make_async_copy(ref, slot, sems.at[k]), row, ref.shape[0]))
            row += ref.shape[0]
        for copy, _, _ in copies:
            copy.start()
        for copy, row, rows in copies:
            copy.wait()
            multiply(right_ref[row : row + rows, :], left_ref, product_ref, first_block, at + row)

    @pl.when(step > 0)
    def _():
        multiply(right_ref[...], left_ref, product_ref, first_block, at)


def early_kernel(count, left_ref, *refs):
    owns, (out_ref, right_ref, sems) = refs[:count], refs[count:]
    multiply_pieces([ref.at[0] for ref in owns], right_ref, sems, left_ref, out_ref, 0, 0)


def early_products(left, owns):
    groups, width, _ = left.shape
    examples = groups * STEP
    total = sum(o.shape[1] for o in owns)
    return pl.pallas_call(
        functools.partial(early_kernel, len(owns)),
        out_shape=jax.ShapeDtypeStruct((examples // BLOCK, total, BLOCK), f32),
        grid=(groups,),
        in_specs=[pl.BlockSpec((1, width, STEP), lambda i: (i, 0, 0))]
        + [pl.BlockSpec(memory_space=pl.ANY)] * len(owns),
        out_specs=pl.BlockSpec((STEP // BLOCK, total, BLOCK), lambda i: (i, 0, 0)),
        scratch_shapes=[
            pltpu.VMEM((total, width), bf16),
            pltpu.SemaphoreType.DMA((len(owns),)),
        ],
        compiler_params=params(32 * 2**20),
        cost_estimate=BRIEF,
    )(left, *owns)


def tiles_kernel(count, block_ref, row_ref, left_ref, early_ref, *refs):
    rights = refs[:count]
    keep_ref, give_ref, product_ref, right_ref, sems, early_sem = refs[count:]
    step = pl.program_id(0)
    early = early_ref.shape[1]
    early_copy = pltpu.make_async_copy(early_ref, product_ref.at[:, pl.ds(0, early)], early_sem)

    @pl.when(step == 0)
    def _():
        early_copy.start()

    block = step * (left_ref.shape[2] // BLOCK)
    multiply_pieces(rights, right_ref, sems, left_ref, product_ref, block, early)

    @pl.when(step == pl.num_programs(0) - 1)
    def _():
        early_copy.wait()
        rows = keep_ref.shape[1]
        for out_ref, base in ((give_ref, keep_ref.shape[0]), (keep_ref, 0)):
            for q in range(out_ref.shape[0]):
                row = pl.multiple_of(row_ref[base + q], 16)
                out_ref[q] = product_ref[block_ref[base + q], pl.ds(row, rows), :]


def tiles(left, early, rights, rows, block, row):
    groups, width, _ = left.shape
    examples = groups * STEP
    total = sum(r.shape[0] for r in rights)
    pairs = block.shape[0]
    out = jax.ShapeDtypeStruct((pairs // 2, rows, BLOCK), f32)
    out_spec = pl.BlockSpec(out.shape, lambda i, *_: (0, 0, 0))
    return pl.pallas_call(
        functools.partial(tiles_kernel, len(rights)),
        out_shape=(out, out),
        grid_spec=pltpu.PrefetchScalarGridSpec(
            num_scalar_prefetch=2,
            grid=(examples // STEP,),
            in_specs=[pl.BlockSpec((1, width, STEP), lambda i, *_: (i, 0, 0))]
            + [pl.BlockSpec(memory_space=pl.ANY)] * (1 + len(rights)),
            out_specs=(out_spec, out_spec),
            scratch_shapes=[
                pltpu.VMEM((examples // BLOCK, early.shape[1] + total, BLOCK), f32),
                pltpu.VMEM((total, width), bf16),
                pltpu.SemaphoreType.DMA((len(rights),)),
                pltpu.SemaphoreType.DMA(()),
            ],
        ),
        compiler_params=params(32 * 2**20),
        cost_estimate=BRIEF,
    )(block, row, left, early, *rights)


def merge_kernel(keep_ref, got_ref, own_ref, *send_refs):
    per = own_ref.shape[0]
    own_ref[...] = keep_ref[:per] + got_ref[:per]
    for k, ref in enumerate(send_refs, 1):
        ref[...] = (keep_ref[k * per : (k + 1) * per] + got_ref[k * per : (k + 1) * per]).astype(bf16)


def merge(keep, got):
    shape = (keep.shape[0] // SIDE, *keep.shape[1:])
    return pl.pallas_call(
        merge_kernel,
        out_shape=(jax.ShapeDtypeStruct(shape, f32),)
        + (jax.ShapeDtypeStruct(shape, bf16),) * (SIDE - 1),
        compiler_params=params(32 * 2**20),
        cost_estimate=BRIEF,
    )(keep, got)


def finish_kernel(*refs):
    ins, out_ref = refs[:-1], refs[-1]
    for k in range(out_ref.shape[0]):
        columns = []
        for at in range(0, len(ins), SIDE):
            total = ins[at][k]
            for ref in ins[at + 1 : at + SIDE]:
                total = total + ref[k].astype(f32)
            columns.append(total)
        out_ref[k] = jnp.concatenate(columns, axis=0).T


def finish(parts):
    ins = [x for part in parts for x in part]
    return pl.pallas_call(
        finish_kernel,
        out_shape=jax.ShapeDtypeStruct((ins[0].shape[0], BLOCK, BLOCK), f32),
        compiler_params=params(16 * 2**20),
    )(*ins)


def shift(array, leg, d):
    pairs = []
    for y in range(SIDE):
        for x in range(SIDE):
            for i in range(2 * SIDE):
                dy, dx = (d, 0) if leg == i % 2 else (0, d)
                to = (y + dy) % SIDE * SIDE + (x + dx) % SIDE
                pairs.append(((y * SIDE + x) * 2 * SIDE + i, to * 2 * SIDE + i))
    return lax.ppermute(array, ("ex", "lay"), pairs)


def swap_cores(array):
    return lax.ppermute(array, "lay", [(i, i ^ 1) for i in range(2 * SIDE)])


def shift_z(array, dz):
    pairs = [(z * 2 + c, (z + dz) % SIDE * 2 + c) for z in range(SIDE) for c in range(2)]
    return lax.ppermute(array, "lay", pairs)


def after(value, other):
    return lax.optimization_barrier((value, other))[0]


STEPS = (1, 3, 2)


def on_device(grads, prec_in, prec_out, requests, pairs):
    grads, prec_in, prec_out = grads[0], prec_in[0], prec_out[0]
    examples, width = grads.shape
    block_count = examples // BLOCK
    blocks = grads.reshape(block_count, BLOCK, width)
    member, layer = lax.axis_index("ex"), lax.axis_index("lay")
    my_y, my_x = member // SIDE, member % SIDE
    my_z, my_core = layer // 2, layer % 2

    wanted = lax.dynamic_index_in_dim(requests, member, axis=1, keepdims=False).reshape(SIDE, SIDE)
    wanted = jnp.concatenate([wanted, wanted], 0)
    wanted = jnp.concatenate([wanted, wanted], 1)
    wanted = lax.dynamic_slice(wanted, (my_y, my_x), (SIDE, SIDE))

    wanted = jnp.where(my_core == 0, wanted, wanted.T)

    (row1, rows1), (row2, rows2) = PARTS
    one = {}
    for d in STEPS:
        (bundle,) = gather(blocks, [(wanted[d], row1, rows1)])
        one[d] = shift(bundle, 0, d)
    one[0], *bundles = gather(
        blocks, [(wanted[0], row1, rows1)] + [(wanted[d], row2, rows2) for d in range(SIDE)]
    )
    left = left_transposed(after(grads, bundles), prec_in, prec_out)
    bundles = after(bundles, (left, one[1]))
    two = {d: shift(bundles[d], 0, d) for d in STEPS} | {0: bundles[0]}
    one = [one[d] for d in range(SIDE)]
    turned = dict(enumerate(turn(one), 1))
    one_in = [shift(after(turned[k], two[1]), 1, k) for k in STEPS]
    early_one = early_products(after(left, turned), one)
    two = after([two[d] for d in range(SIDE)], early_one)
    turned = dict(enumerate(turn(two), 1))
    turned, early_one = lax.optimization_barrier((turned, early_one))
    early_two = early_products(left, after(two, turned))
    gate = one_in[0]
    two_in = [shift(after(turned[k], gate), 1, k) for k in STEPS]
    one_in = after(one_in, early_two)

    first = pairs[:, 0] - member * block_count
    dy = (my_y - pairs[:, 1] // SIDE) % SIDE
    dx = (my_x - pairs[:, 1] % SIDE) % SIDE
    leg0, leg1 = jnp.where(my_core == 0, dy, dx), jnp.where(my_core == 0, dx, dy)
    place = sum(jnp.where(leg1 == k, at, 0) for at, k in enumerate(STEPS, 1))
    listed = jnp.stack([first, place * SIDE + leg0])
    listed = listed.reshape(2, SIDE, 2, -1)
    listed = jnp.concatenate([listed, listed], 1)
    listed = lax.dynamic_slice_in_dim(listed, my_z, SIDE, 1)
    listed = jnp.where(my_core == 0, listed, listed[:, :, ::-1])
    listed = listed.transpose(0, 2, 1, 3).reshape(2, -1)

    sums = []
    for (_, rows), early in zip(PARTS, (early_one, early_two)):
        got = two_in if sums else one_in
        rest = [v.reshape(-1, width) for v in got]
        if sums:
            rest = after(rest, sums[-1])
        keep, give = tiles(left, early, rest, rows, listed[0], listed[1] * rows)
        mine, *sends = merge(keep, swap_cores(give))
        sums.append([mine] + [shift_z(s, k) for k, s in enumerate(sends, 1)])
    return finish(sums)


def solution(mesh):
    placed = (P("lay", "ex", None), P("lay", None, None), P("lay", None, None), P(), P("ex", None))
    return jax.shard_map(
        on_device,
        mesh=mesh,
        in_specs=placed,
        out_specs=P(("ex", "lay"), None, None),
        check_vma=False,
    )
```
